128 devices in a mesh: grp: 4 (over y), enc: 32 (over x, z, core).
Axes of the slice: x: 4, y: 4, z: 4, core: 2. Of those that a mesh axis runs over, the one named last changes fastest.
Arguments:
- patches: bfloat16 [32768, 1280], P(('grp', 'enc')), may hold values from -16 to 16
- ln_gain: float32 [1280], replicated, may hold values from 0.1 to 1.9
- qkv_weight: bfloat16 [1280, 3840], P('enc')
- out_weight: bfloat16 [1280, 1280], P('enc'), may hold values from -0.15625 to 0.15625
- image_counts: int32 [128, 4], P(('grp', 'enc')), may hold values from 1 to 128, as said below
- window_order: int32 [256, 128], P(('grp', 'enc')), may hold values from 0 to 255, as said below
- owner_map: int32 [32768, 1], P(('grp', 'enc')), may hold values from 0 to 127; in each aligned block of 256 rows (0 to 255, 256 to 511, ...) at most 4 rows name the same one
- owner_grads: bfloat16 [65536, 1280], P(('grp', 'enc')), may hold values from -6 to 6
Outputs:
- owner_rows: bfloat16 [65536, 1280], P(('grp', 'enc'))
- patch_grads: bfloat16 [32768, 1280], P(('grp', 'enc'))
- qkv_grad: float32 [1280, 3840], P('enc')
- out_grad: float32 [1280, 1280], P('enc')
The draws below stay inside these ranges and needn't reach their ends.
Inputs may be any that keep to these rules, and one draw needn't show every extreme that they name: `image_counts`: each pack's 4 counts sum to 256 and its largest count is exactly 128. `window_order`: each pack's entries, read in order, are a permutation of 0 to 255 that lists all rows of its first image, then all rows of its second, and so on; within an image the order is arbitrary. `owner_map`: in each pack no owner is named by more than 4 of the pack's rows, a bound that some block reaches.
All inputs are finite; a program needn't handle non-finite values.
Results may differ from the reference program's by a relative error of at most 0.024.
Values may be sent and summed in bfloat16 or wider, within the bound.
No kernel may reach another device: no remote copies, remote signals or barrier semaphores. Data moves between devices by JAX's collectives and lax.ppermute only.
A program may use at most 128 MiB of HBM per device.

```python
import math
import jax
import jax.numpy as jnp
import numpy as np
from jax import lax

D = 1280
HEADS = 16
HD = 80
WIN = 128
IMGS = 4
ROWS = 256
MOST = 128
CAP = 4
TOKENS = 32768
SLOTS = 512
DEVICES = 128


def packing(key):
    weight_key = jax.random.fold_in(key, 101)
    place_key = jax.random.fold_in(key, 102)
    shuffle_key = jax.random.fold_in(key, 103)
    extra_rows = ROWS - MOST - (IMGS - 1)
    portions = jax.random.randint(weight_key, (DEVICES, IMGS - 1), 1, 64).astype(jnp.int32)
    running = jnp.cumsum(portions, axis=1)
    cut_points = extra_rows * running // running[:, -1:]
    starts = jnp.concatenate([jnp.zeros((DEVICES, 1), jnp.int32), cut_points[:, :-1]], axis=1)
    others = (1 + cut_points - starts).astype(jnp.int32)
    lengths = jnp.concatenate([jnp.full((DEVICES, 1), MOST, jnp.int32), others], axis=1)
    placing = jax.vmap(lambda subkey: jax.random.permutation(subkey, IMGS))(jax.random.split(place_key, DEVICES))
    lengths = jnp.take_along_axis(lengths, placing, axis=1)
    image_ends = jnp.cumsum(lengths, axis=1)
    image_ids = jnp.sum(jnp.arange(ROWS, dtype=jnp.int32)[None, :, None] >= image_ends[:, None, :], axis=2).astype(jnp.int32)
    shuffle = jax.vmap(lambda subkey: jax.random.permutation(subkey, ROWS))(jax.random.split(shuffle_key, DEVICES)).astype(jnp.int32)
    sort_key = image_ids * ROWS + shuffle
    row_order = jnp.argsort(sort_key, axis=1, stable=True)
    return (lengths.astype(jnp.int32), row_order.astype(jnp.int32))


def draw_image_counts(key, part):
    lengths, row_order = packing(key)
    return lengths


def draw_window_order(key, part):
    lengths, row_order = packing(key)
    return row_order.reshape(TOKENS // WIN, WIN)


def draw_patches(key, part):
    key = jax.random.fold_in(key, 7)
    fields = jnp.clip(jax.random.normal(key, (DEVICES, ROWS, D), jnp.float32), -16.0, 16.0)
    return fields.reshape(TOKENS, D).astype(jnp.bfloat16)


def draw_qkv_weight(key, part):
    key = jax.random.fold_in(key, 13)
    matrix_key = jax.random.fold_in(key, 0)
    bound = 8.0 * D ** (-0.5)
    matrix = jax.random.normal(matrix_key, (D, 3 * D), jnp.float32) * D ** (-0.5)
    return jnp.clip(matrix, -bound, bound).astype(jnp.bfloat16)


def shard_levels(rng, extent, cuts, smallest, high):
    level, own = 1.0, jax.random.fold_in(rng, 6)
    for axis_at, parts in cuts:
        steps = jnp.exp(jax.random.uniform(jax.random.fold_in(own, axis_at), (parts,), jnp.float32, smallest / len(cuts), high / len(cuts)))
        level = level * jnp.repeat(steps, extent[axis_at] // parts).reshape([-1 if axis == axis_at else 1 for axis in range(len(extent))])
    return level


def deal_out(rng, own, number, rows, number_of, top, most, lean):
    order = jax.random.permutation(rng, number_of)
    heavy_load, usual = shares(number_of, rows * top, most, lean, True), shares(number_of, rows * top, most, lean, False)
    places = jnp.arange(number_of)

    def named(tallies, turn):
        used = int((tallies > 0).sum())
        fixed = max(1, used // 4)
        passed = fixed + (places - fixed + turn * (used - fixed)) % max(1, number_of - fixed)
        return jnp.zeros((number_of,), jnp.int32).at[order[jnp.where(places < fixed, places, passed)]].set(jnp.asarray(tallies, jnp.int32))

    tallies = jnp.where(number % 4 == 0, named(heavy_load, number // 4), named(usual, number - number // 4 - 1))
    mixed = jax.random.permutation(jax.random.fold_in(own, 3), number_of)
    giver, sink = mixed[0:number_of // 2 * 2:2], mixed[1:number_of // 2 * 2:2]
    room = jnp.minimum(tallies[giver] - 1, most - tallies[sink]) // 2
    room = jnp.where((giver == order[0]) | (sink == order[0]) | (tallies[sink] == 0), 0, jnp.maximum(room, 0))
    passed = jax.random.randint(jax.random.fold_in(own, 4), (number_of // 2,), 0, 1 << 20) % (room + 1)
    tallies = tallies.at[giver].add(-passed).at[sink].add(passed)
    items = jnp.searchsorted(jnp.cumsum(tallies), jnp.arange(rows * top), side="right").astype(jnp.int32)
    listing = items.reshape(top, rows).T
    listing = listing[jax.random.permutation(jax.random.fold_in(own, 1), rows)]
    turn = jax.random.randint(jax.random.fold_in(own, 2), (rows, 1), 0, top)
    return jnp.take_along_axis(listing, (jnp.arange(top)[None, :] + turn) % top, axis=1)


def shares(number_of, total, most, skew, full):
    loads = [(1 << 20) // math.isqrt(grade ** skew) + 1 for grade in range(1, number_of + 1)]
    largest = most if full else min(most, max(-(-total // number_of), total * loads[0] // sum(loads)))
    least = 1 if total - largest >= number_of - 1 else 0
    counts, surplus = [largest] + [least] * (number_of - 1), total - largest - least * (number_of - 1)
    while surplus > 0:
        candidates = [i for i in range(1, number_of) if counts[i] < largest] or [i for i in range(1, number_of) if counts[i] < most]
        mass, budget = sum([loads[i] for i in candidates]), surplus
        for i in candidates:
            more = min(most - counts[i], max(1, budget * loads[i] // mass), surplus)
            counts[i] = counts[i] + more
            surplus = surplus - more
    return np.array(counts)


def gaussian(key, extent, deviation, most, pieces=(), kind=jnp.bfloat16):
    level = shard_levels(key, extent, pieces, -0.22, 0.18) if pieces else 1.0
    entries = jax.random.normal(key, extent, jnp.float32) * deviation * level
    return jnp.minimum(jnp.maximum(entries, -most), most).astype(kind)


def setup_inputs(seed: int = 0) -> dict:
    splits = jax.random.split(jax.random.key(seed), 9)
    patches = draw_patches(jax.random.fold_in(splits[8], 71), 0)
    ln_gain = jnp.clip(1.0 + 0.18 * jax.random.normal(splits[1], (D,), jnp.float32), 0.1, 1.9)
    qkv_weight = draw_qkv_weight(jax.random.fold_in(splits[8], 71), 0)
    out_weight = gaussian(splits[3], (D, D), D ** -0.5, 0.15625, ((0, 32),))
    image_counts = draw_image_counts(jax.random.fold_in(splits[8], 71), 0)
    window_order = draw_window_order(jax.random.fold_in(splits[8], 71), 0)
    owner_map_keys = jax.random.split(jax.random.fold_in(splits[6], 1), TOKENS // ROWS)
    owner_map_turns = jax.random.permutation(jax.random.fold_in(splits[6], 3), TOKENS // ROWS)
    owner_map = jax.vmap(lambda own, number: deal_out(jax.random.fold_in(splits[6], 2), own, number, ROWS, DEVICES, 1, CAP, 2))(owner_map_keys, owner_map_turns).reshape((TOKENS, 1))
    owner_grads = gaussian(splits[7], (DEVICES * SLOTS, D), 1.0, 6.0, ((0, 128),))
    return {"patches": patches, "ln_gain": ln_gain, "qkv_weight": qkv_weight, "out_weight": out_weight, "image_counts": image_counts, "window_order": window_order, "owner_map": owner_map, "owner_grads": owner_grads}


EPSILON = 1e-06

def rms_norm(device_rows):
    widened = device_rows.astype(jnp.float32)
    inverse_spread = lax.rsqrt(lax.optimization_barrier(jnp.mean(widened * widened, axis=-1, keepdims=True)) + EPSILON)
    return (widened * inverse_spread, inverse_spread)

def softmax_probs(query_rows, key_rows, allowed, score_scale):
    scores = jnp.einsum('wihd,wjhd->whij', query_rows.astype(jnp.float32), key_rows.astype(jnp.float32)) * score_scale
    scores = jnp.where(allowed[:, None], scores, -1e+30)
    row_max = lax.optimization_barrier(jnp.max(scores, axis=-1, keepdims=True))
    expanded = jnp.exp(scores - row_max)
    return expanded / lax.optimization_barrier(jnp.sum(expanded, axis=-1, keepdims=True))

def reference(patches, ln_gain, qkv_weight, out_weight, image_counts, window_order, owner_map, owner_grads):
    windows = ROWS // WIN
    score_scale = HD ** (-0.5)
    owner_width = DEVICES * CAP

    def one_pack(summed, inputs):
        pack_rows, lengths, row_order, owners, pack = inputs
        image_ends = jnp.cumsum(lengths)
        image_of = lax.optimization_barrier(jnp.sum(jnp.arange(ROWS, dtype=jnp.int32)[:, None] >= image_ends[None, :], axis=1)).astype(jnp.int32)
        image_window = image_of[row_order].reshape(windows, WIN)
        allowed = image_window[:, :, None] == image_window[:, None, :]
        onehot = (owners[:, None] == jnp.arange(DEVICES, dtype=jnp.int32)[None, :]).astype(jnp.int32)
        before = jnp.cumsum(onehot, axis=0) - onehot
        slot_index = lax.optimization_barrier(jnp.sum(before * onehot, axis=1))
        target = (owners * owner_width + pack * CAP + slot_index).astype(jnp.int32)
        target_window = target[row_order]
        ordered = pack_rows[row_order]
        scaled, inverse_spread = rms_norm(ordered)
        normed = (scaled * ln_gain).astype(jnp.bfloat16)
        qkv = jnp.dot(normed, qkv_weight, preferred_element_type=jnp.float32).astype(jnp.bfloat16)
        query_rows = qkv[:, :D].reshape(windows, WIN, HEADS, HD)
        key_rows = qkv[:, D:2 * D].reshape(windows, WIN, HEADS, HD)
        value_rows = qkv[:, 2 * D:].reshape(windows, WIN, HEADS, HD)
        attn_probs = softmax_probs(query_rows, key_rows, allowed, score_scale)
        probs_bf16 = attn_probs.astype(jnp.bfloat16)
        attended = jnp.einsum('whij,wjhd->wihd', probs_bf16.astype(jnp.float32), value_rows.astype(jnp.float32))
        attended = attended.astype(jnp.bfloat16).reshape(ROWS, D)
        embeds = (ordered.astype(jnp.float32) + jnp.dot(attended, out_weight, preferred_element_type=jnp.float32)).astype(jnp.bfloat16)
        grad_embeds = owner_grads[target_window]
        grad_attended = jnp.dot(grad_embeds, out_weight.T, preferred_element_type=jnp.float32).astype(jnp.bfloat16)
        grad_heads = grad_attended.reshape(windows, WIN, HEADS, HD).astype(jnp.float32)
        grad_value = jnp.einsum('whij,wihd->wjhd', probs_bf16.astype(jnp.float32), grad_heads).astype(jnp.bfloat16)
        grad_probs = jnp.einsum('wihd,wjhd->whij', grad_heads, value_rows.astype(jnp.float32))
        inner = lax.optimization_barrier(jnp.sum(attn_probs * grad_probs, axis=-1, keepdims=True))
        grad_scores = (attn_probs * (grad_probs - inner) * score_scale).astype(jnp.bfloat16).astype(jnp.float32)
        grad_query = jnp.einsum('whij,wjhd->wihd', grad_scores, key_rows.astype(jnp.float32)).astype(jnp.bfloat16)
        grad_key = jnp.einsum('whij,wihd->wjhd', grad_scores, query_rows.astype(jnp.float32)).astype(jnp.bfloat16)
        grad_qkv = jnp.concatenate([grad_query.reshape(ROWS, D), grad_key.reshape(ROWS, D), grad_value.reshape(ROWS, D)], axis=1)
        grad_normed = jnp.dot(grad_qkv, qkv_weight.T, preferred_element_type=jnp.float32).astype(jnp.bfloat16)
        scaled_grad = grad_normed.astype(jnp.float32) * ln_gain
        grad_layer = (scaled_grad - scaled * lax.optimization_barrier(jnp.mean(scaled_grad * scaled, axis=-1, keepdims=True))) * inverse_spread
        window_grads = (grad_embeds.astype(jnp.float32) + grad_layer).astype(jnp.bfloat16)
        patch_grads = jnp.zeros((ROWS, D), jnp.bfloat16).at[row_order].set(window_grads)
        term = jnp.concatenate([jnp.dot(normed.T, grad_qkv, preferred_element_type=jnp.float32), jnp.dot(attended.T, grad_embeds, preferred_element_type=jnp.float32)], axis=1)
        rounded = lax.optimization_barrier(term.astype(jnp.bfloat16)).astype(jnp.float32)
        return (summed + rounded, (embeds, target_window, patch_grads))
    inputs = (patches.reshape(DEVICES, ROWS, D), image_counts, window_order.reshape(DEVICES, ROWS), owner_map.reshape(DEVICES, ROWS), jnp.arange(DEVICES, dtype=jnp.int32))
    summed, stacked = lax.scan(one_pack, jnp.zeros((D, 4 * D), jnp.float32), inputs)
    embeds_all, targets_all, grads_all = stacked
    owner_rows = jnp.zeros((DEVICES * owner_width, D), jnp.bfloat16).at[targets_all.reshape(-1)].set(embeds_all.reshape(-1, D))
    grad_factor = 1.0 / math.sqrt(TOKENS)
    qkv_grad = summed[:, :3 * D] * grad_factor
    out_grad = summed[:, 3 * D:] * grad_factor
    return (owner_rows, grads_all.reshape(TOKENS, D), qkv_grad, out_grad)
```

```python
import math

import jax
import jax.numpy as jnp
from jax import lax
from jax.experimental import pallas as pl
from jax.experimental.pallas import tpu as pltpu
from jax.sharding import PartitionSpec as P

HEADS = 16
HD = 80
WIN = 128
EPSILON = 1e-06
D = 1280
ROWS = 256
HALF = 640
HPC = HEADS // 2
BF = jnp.bfloat16
F32 = jnp.float32
VMEM_LIMIT = 58 * 1024 * 1024
STEPS = (0, 1, -1, 2)


def ring(axis, step):
    pairs = []
    for x in range(4):
        for z in range(4):
            for c in range(2):
                to = ((x + step) % 4, z) if axis == "x" else (x, (z + step) % 4)
                pairs.append(((x * 4 + z) * 2 + c, (to[0] * 4 + to[1]) * 2 + c))
    return pairs


def hop(value, axis, step):
    if axis == "y":
        return lax.ppermute(value, "grp", [(i, (i + step) % 4) for i in range(4)])
    return lax.ppermute(value, "enc", ring(axis, step))


def to_sibling(value):
    return lax.ppermute(value, "enc", [(i, i ^ 1) for i in range(32)])


def to_halves(value, same, back=False):
    pairs = []
    for x in range(4):
        for z in range(4):
            for c in range(2):
                half = c if same else 1 - c
                source = (x * 4 + z) * 2 + c
                target = ((x % 2 + 2 * half) * 4 + z) * 2 + x // 2
                pairs.append((target, source) if back else (source, target))
    return lax.ppermute(value, "enc", pairs)


def gather_line(shard, first):
    behind = hop(shard, first, 1)
    ahead = hop(shard, first, -1)
    across = hop(shard, first, 2)
    return jnp.stack([shard, ahead, behind, across])


def gather_rest(line, second):
    line_behind = hop(line, second, 1)
    line_ahead = hop(line, second, -1)
    far_low = hop(line_behind[:2], second, 1)
    far_high = hop(line_ahead[2:], second, -1)
    return line, line_ahead, line_behind, far_low, far_high


def add(*values):
    total = values[0].astype(F32)
    for v in values[1:]:
        total = total + v.astype(F32)
    return total


def scatter_first(up, down, axis):
    return hop(up, axis, 1), hop(down, axis, -1)


def scatter_second(own, from_up, from_down, next_up, next_down, first, second):
    last_up = hop(add(next_up, from_up[:2]).astype(BF), first, 1)
    last_down = hop(add(next_down, from_down[:2]).astype(BF), first, -1)
    total = jnp.concatenate([add(own[:2], last_up, from_down[2:]), add(own[2:], from_up[2:], last_down)])
    rounded = total.astype(BF)
    one = hop(rounded[1], second, 1)
    two = hop(rounded[2], second, -1)
    three = hop(rounded[3], second, 2)
    return add(total[0], one, two, three)


def dot(a, b):
    return jnp.dot(a, b, preferred_element_type=F32)


def dot_nt(a, b):
    return lax.dot_general(a, b, (((1,), (1,)), ((), ())), preferred_element_type=F32)


def dot_tn(a, b):
    return lax.dot_general(a, b, (((0,), (0,)), ((), ())), preferred_element_type=F32)


def call(kernel, outs, ins, in_spaces, out_spaces=None, scratch=(), us=3):
    spaces = {"v": pltpu.VMEM, "s": pltpu.SMEM, "a": pltpu.HBM}
    out_spaces = out_spaces or "v" * len(outs)
    return pl.pallas_call(
        kernel,
        out_shape=[jax.ShapeDtypeStruct(s, t) for s, t in outs],
        in_specs=[pl.BlockSpec(memory_space=spaces[c]) for c in in_spaces],
        out_specs=[pl.BlockSpec(memory_space=spaces[c]) for c in out_spaces],
        scratch_shapes=list(scratch),
        compiler_params=pltpu.CompilerParams(vmem_limit_bytes=VMEM_LIMIT),
        cost_estimate=pl.CostEstimate(flops=us * 10**9, bytes_accessed=us * 3 * 10**6, transcendentals=0),
    )(*ins)


def prepare_kernel(counts, patches, gain, order, owners, naug, gather, ordered):
    rows = lax.broadcasted_iota(jnp.int32, (ROWS, ROWS), 1)
    perm = (order[...] == rows).astype(BF)
    row = lax.broadcasted_iota(jnp.int32, (ROWS, 128), 0)
    lane = lax.broadcasted_iota(jnp.int32, (ROWS, 128), 1)
    image = jnp.zeros((ROWS, 128), jnp.int32)
    end = 0
    for k in range(4):
        end = end + counts[0, k]
        image = image + (row >= end).astype(jnp.int32)
    kinds = dot(perm, (image == lane).astype(BF)).astype(BF)
    named = (owners[...] == lane).astype(BF)
    earlier = (rows < lax.broadcasted_iota(jnp.int32, (ROWS, ROWS), 0)).astype(BF)
    before = dot(earlier, named)
    slot = jnp.sum(before * named.astype(F32), axis=1, keepdims=True).astype(jnp.int32)
    target = owners[...] * 4 + slot
    slots = lax.broadcasted_iota(jnp.int32, (ROWS, 512), 1)
    gather[...] = dot(perm, (target == slots).astype(BF)).astype(BF)
    rowsw = dot(perm, patches[...])
    ordered[...] = rowsw.astype(BF)
    spread = lax.rsqrt(jnp.mean(rowsw * rowsw, axis=1, keepdims=True) + EPSILON)
    naug[:, :D] = (rowsw * spread * gain[...]).astype(BF)
    naug[:, D:] = kinds


def pick_kernel(gather, returned, out):
    out[...] = dot(gather[...], returned[...]).astype(BF)


class Copies:
    def __init__(self, sems):
        self.sems, self.used = sems, 0

    def make(self, src, dst):
        self.used += 1
        return pltpu.make_async_copy(src, dst, self.sems.at[self.used - 1])

    def start(self, src, dst):
        copy = self.make(src, dst)
        copy.start()
        return copy


def wait_all(copies):
    for c in copies:
        c.wait()


def assemble(place, parts, first, copy_one, scatter=False):
    line, ahead, behind, low, high = parts
    x, z = place[0], place[1]
    copies = []
    for i, step in enumerate(STEPS):
        for j, inner in enumerate(STEPS):
            if step == 0:
                ref = line.at[j]
            elif step == 1:
                ref = ahead.at[j]
            elif step == -1:
                ref = behind.at[j]
            else:
                ref = low.at[j] if j < 2 else high.at[j - 2]
            if scatter:
                ref = pieces_at(*parts, step, j)
            if first == "z":
                dx, dz = step, inner
            else:
                dx, dz = inner, step
            copies += copy_one(ref, (x + dx + 4) % 4, (z + dz + 4) % 4)
    return copies


def at_rows(index, size):
    return pl.ds(pl.multiple_of(index * size, size), size)


def forward_kernel(place, own, sib, a0, a1, a2, a3, a4, b0, b1, b2, b3, b4,
                   probs_out, qkv_out, attended, mine, theirs,
                   wqkv, wout, both, scores, probs, qkv, sems):
    copies = Copies(sems)
    from_a = assemble(
        place, (a0, a1, a2, a3, a4), "z",
        lambda ref, x, z: [copies.start(ref, wqkv.at[at_rows(x * 4 + z, 80), pl.ds(0, 1280)])],
    )
    from_b = assemble(
        place, (b0, b1, b2, b3, b4), "x",
        lambda ref, x, z: [
            copies.start(ref.at[:, pl.ds(0, 640)], wqkv.at[at_rows(x * 4 + z, 80), pl.ds(1280, 640)])
        ],
    )
    from_b_out = assemble(
        place, (b0, b1, b2, b3, b4), "x",
        lambda ref, x, z: [
            copies.start(ref.at[:, pl.ds(640, 640)], wout.at[at_rows((x % 2) * 4 + z, 80), at_rows(x // 2, 640)])
        ],
    )
    both[:ROWS, :] = own[:, :D]
    both[ROWS:, :] = sib[:, :D]
    wait_all(from_a)

    def project(col):
        qkv[:, col] = dot(both[...], wqkv[:, col]).astype(BF)

    @pl.loop(0, 5)
    def _(t):
        project(at_rows(t, 256))

    wait_all(from_b)
    project(pl.ds(1280, 256))
    project(pl.ds(1536, 256))
    project(pl.ds(1792, 128))
    out_copies = [copies.start(qkv, qkv_out)]
    scale = HD ** (-0.5)

    @pl.loop(0, 4)
    def _(w):
        rows = at_rows(w, WIN)
        local = at_rows(w % 2, WIN)
        kinds = jnp.where(w < 2, own[local, D:].astype(F32), sib[local, D:].astype(F32)).astype(BF)
        allowed = dot_nt(kinds, kinds) > 0.5
        for h in range(HPC):
            q = qkv[rows, h * HD:(h + 1) * HD]
            k = qkv[rows, HALF + h * HD:HALF + (h + 1) * HD]
            scores[h] = dot_nt(k, q)
        for h in range(HPC):
            s = jnp.where(allowed, scores[h] * scale, -1e30)
            e = jnp.exp(s - jnp.max(s, axis=0, keepdims=True))
            probs[w, h] = e * (1.0 / jnp.sum(e, axis=0, keepdims=True))
        for h in range(HPC):
            v = qkv[rows, 2 * HALF + h * HD:2 * HALF + (h + 1) * HD]
            attended[rows, h * HD:(h + 1) * HD] = dot_tn(probs[w, h].astype(BF), v).astype(BF)

    out_copies.append(copies.start(probs, probs_out))
    wait_all(from_b_out)

    @pl.loop(0, 5)
    def _(t):
        col = at_rows(t, 256)
        part = dot(attended[...], wout[:, col])
        mine[:, col] = part[:ROWS]
        theirs[:, col] = part[ROWS:].astype(BF)

    wait_all(out_copies)


def embed_kernel(mine, theirs, ordered, gather, out):
    embeds = (ordered[...].astype(F32) + (mine[...] + theirs[...].astype(F32))).astype(BF)
    out[...] = dot_tn(gather[...], embeds).astype(BF)


def turn_kernel(own, sib, out):
    out[:, :ROWS] = own[:, :D].T
    out[:, ROWS:] = sib[:, :D].T


def pieces_at(own, up, down, next_up, next_down, step, inner):
    if step == 0:
        return own.at[inner]
    if step == 1:
        return next_up.at[inner] if inner < 2 else up.at[inner]
    if step == -1:
        return down.at[inner + 2] if inner < 2 else next_down.at[inner - 2]
    return up.at[inner] if inner < 2 else down.at[inner - 2]


def backward_kernel(place, gown, gsib, b0, b1, b2, b3, b4, normed_hbm, probs_hbm, qkv_hbm, attended_hbm,
                    gqkv_out, aown, aup, adown, alow, ahigh, bown, bup, bdown, blow, bhigh,
                    wout, grads, gatt, terms, oterms, scores, small, normed_t, attended, attended_t,
                    probs, qkv, gqkv, sems):
    copies = Copies(sems)
    grads_in = [
        copies.start(gown, grads.at[pl.ds(0, ROWS)]),
        copies.start(gsib, grads.at[pl.ds(ROWS, ROWS)]),
    ]
    grads_in += assemble(
        place, (b0, b1, b2, b3, b4), "x",
        lambda ref, x, z: [
            copies.start(ref.at[:, pl.ds(640, 640)], wout.at[at_rows((x % 2) * 4 + z, 80), at_rows(x // 2, 640)])
        ],
    )
    first_in = [copies.start(qkv_hbm, qkv), copies.start(probs_hbm, probs)]
    second_in = [copies.start(attended_hbm, attended), copies.start(normed_hbm, normed_t)]
    wait_all(grads_in)
    gatt[...] = dot_nt(grads[...], wout[...]).astype(BF)
    scale = HD ** (-0.5)
    wait_all(first_in)

    @pl.loop(0, 4)
    def _(w):
        rows = at_rows(w, WIN)
        for h in range(HPC):
            a, b = h * HD, (h + 1) * HD
            scores[h] = dot_nt(qkv[rows, 2 * HALF + a:2 * HALF + b], gatt[rows, a:b])
        for h in range(HPC):
            a, b = h * HD, (h + 1) * HD
            gqkv[rows, 2 * HALF + a:2 * HALF + b] = dot(probs[w, h].astype(BF), gatt[rows, a:b]).astype(BF)
        for h in range(HPC):
            p = probs[w, h]
            g = scores[h]
            inner = jnp.sum(p * g, axis=0, keepdims=True)
            small[h] = (p * (g - inner) * scale).astype(BF)
        for h in range(HPC):
            a, b = h * HD, (h + 1) * HD
            gqkv[rows, HALF + a:HALF + b] = dot(small[h], qkv[rows, a:b]).astype(BF)
            gqkv[rows, a:b] = dot_tn(small[h], qkv[rows, HALF + a:HALF + b]).astype(BF)

    out_copies = [copies.start(gqkv, gqkv_out)]
    wait_all(second_in)

    def weigh(col):
        terms[:, col] = dot(normed_t[...], gqkv[:, col]).astype(BF)

    @pl.loop(0, 5)
    def _(t):
        weigh(at_rows(t, 256))

    out_copies += assemble(
        place, (aown, aup, adown, alow, ahigh), "z",
        lambda ref, x, z: [copies.start(terms.at[at_rows(x * 4 + z, 80), pl.ds(0, 1280)], ref)],
        scatter=True,
    )
    weigh(pl.ds(1280, 256))
    weigh(pl.ds(1536, 256))
    weigh(pl.ds(1792, 128))
    out_copies += assemble(
        place, (bown, bup, bdown, blow, bhigh), "x",
        lambda ref, x, z: [
            copies.start(terms.at[at_rows(x * 4 + z, 80), pl.ds(1280, 640)], ref.at[:, pl.ds(0, 640)])
        ],
        scatter=True,
    )
    attended_t[...] = attended[...].T

    @pl.loop(0, 5)
    def _(t):
        col = at_rows(t, 256)
        oterms[:, col] = dot(attended_t[...], grads[:, col]).astype(BF)

    out_copies += assemble(
        place, (bown, bup, bdown, blow, bhigh), "x",
        lambda ref, x, z: [
            copies.start(oterms.at[at_rows((x % 2) * 4 + z, 80), at_rows(x // 2, 640)], ref.at[:, pl.ds(640, 640)])
        ],
        scatter=True,
    )
    wait_all(out_copies)


def norm_grad_kernel(place, gqkv, a0, a1, a2, a3, a4, b0, b1, b2, b3, b4, mine, theirs, wqkv, sems):
    copies = Copies(sems)
    parts = assemble(
        place, (a0, a1, a2, a3, a4), "z",
        lambda ref, x, z: [copies.start(ref, wqkv.at[at_rows(x * 4 + z, 80), pl.ds(0, 1280)])],
    )
    parts += assemble(
        place, (b0, b1, b2, b3, b4), "x",
        lambda ref, x, z: [
            copies.start(ref.at[:, pl.ds(0, 640)], wqkv.at[at_rows(x * 4 + z, 80), pl.ds(1280, 640)])
        ],
    )
    wait_all(parts)
    for t in range(5):
        col = slice(t * 256, (t + 1) * 256)
        part = dot_nt(gqkv[...], wqkv[col, :])
        mine[:, col] = part[:ROWS]
        theirs[:, col] = part[ROWS:].astype(BF)


def finish_kernel(mine, theirs, ordered, gain, grads, order_t, out):
    rows = lax.broadcasted_iota(jnp.int32, (ROWS, ROWS), 0)
    back = (order_t[...] == rows).astype(BF)
    rowsw = ordered[...].astype(F32)
    spread = lax.rsqrt(jnp.mean(rowsw * rowsw, axis=1, keepdims=True) + EPSILON)
    scaled = rowsw * spread
    normed = (mine[...] + theirs[...].astype(F32)).astype(BF).astype(F32)
    u = normed * gain[...]
    layer = (u - scaled * jnp.mean(u * scaled, axis=1, keepdims=True)) * spread
    window = (grads[...].astype(F32) + layer).astype(BF)
    out[...] = dot(back, window).astype(BF)


def body(patches, ln_gain, qkv_weight, out_weight, image_counts, window_order, owner_map, owner_grads):
    index = lax.axis_index("enc")
    x, z, core = index // 8, (index // 2) % 4, index % 2
    place = jnp.stack([x, z])
    gain = ln_gain.reshape(1, D)
    order = window_order.reshape(ROWS, 1)
    order_t = window_order.reshape(1, ROWS)

    first_core = core == 0
    with jax.named_scope("weights"):

        def columns(half):
            return jnp.concatenate([qkv_weight[:, (2 * t + half) * HALF :][:, :HALF] for t in range(3)], axis=1)

        low, high = columns(0), columns(1)
        got = to_sibling(jnp.where(first_core, high, low))
        keep = jnp.where(first_core, low, high)
        out_low, out_high = out_weight[:, :HALF], out_weight[:, HALF:]
        out_same = to_halves(jnp.where(first_core, out_low, out_high), True)
        out_other = to_halves(jnp.where(first_core, out_high, out_low), False)
    with jax.named_scope("weights"):
        shard = jnp.where(first_core, jnp.concatenate([keep, got]), jnp.concatenate([got, keep]))
        out_shard = jnp.where(
            x < 2, jnp.concatenate([out_same, out_other]), jnp.concatenate([out_other, out_same])
        )
        line_a = gather_line(shard[:, : 2 * HALF], "z")
        line_b = gather_line(jnp.concatenate([shard[:, 2 * HALF :], out_shard], axis=1), "x")
        part_a = gather_rest(line_a, "x")
        part_b = gather_rest(line_b, "z")
    with jax.named_scope("prepare"):
        naug, gather, ordered = call(
            prepare_kernel,
            [((ROWS, D + 128), BF), ((ROWS, 512), BF), ((ROWS, D), BF)],
            (image_counts, patches, gain, order, owner_map),
            "svvvv",
        )
        nsib = to_sibling(naug)
        (normed_t,) = call(turn_kernel, [((D, 512), BF)], (naug, nsib), "vv")

    with jax.named_scope("grads_in"):
        owner_grads, part_a, part_b, normed_t = lax.optimization_barrier((owner_grads, part_a, part_b, normed_t))
        returned = lax.all_to_all(owner_grads, ("grp", "enc"), split_axis=0, concat_axis=0, tiled=True)
    with jax.named_scope("forward"):
        probs, qkv, attended, mine, theirs = call(
            forward_kernel,
            [((4, HPC, WIN, WIN), F32), ((512, 3 * HALF), BF), ((512, HALF), BF), ((ROWS, D), F32), ((ROWS, D), BF)],
            (place, naug, nsib, *part_a, *part_b),
            "svv" + "a" * 10,
            "aavvv",
            scratch=[
                pltpu.VMEM((D, 3 * HALF), BF),
                pltpu.VMEM((HALF, D), BF),
                pltpu.VMEM((512, D), BF),
                pltpu.VMEM((HPC, WIN, WIN), F32),
                pltpu.VMEM((4, HPC, WIN, WIN), F32),
                pltpu.VMEM((512, 3 * HALF), BF),
                pltpu.SemaphoreType.DMA((50,)),
            ],
            us=14,
        )
        from_sib = to_sibling(theirs)
        (outgoing,) = call(embed_kernel, [((512, D), BF)], (mine, from_sib, ordered, gather), "vvvv")
    with jax.named_scope("grads_in"):
        returned, _ = lax.optimization_barrier((returned, outgoing))
        (gown,) = call(pick_kernel, [((ROWS, D), BF)], (gather, returned), "vv")
        gsib = to_sibling(gown)
    with jax.named_scope("backward"):
        gown, gsib, outgoing = lax.optimization_barrier((gown, gsib, outgoing.reshape(128, 4, D)))
        pieces = [((4, 80, D), BF)] * 3 + [((2, 80, D), BF)] * 2
        gqkv, *terms = call(
            backward_kernel,
            [((512, 3 * HALF), BF)] + pieces + pieces,
            (place, gown, gsib, *part_b, normed_t, probs, qkv, attended),
            "s" + "a" * 11,
            "a" * 11,
            scratch=[
                pltpu.VMEM((HALF, D), BF),
                pltpu.VMEM((512, D), BF),
                pltpu.VMEM((512, HALF), BF),
                pltpu.VMEM((D, 3 * HALF), BF),
                pltpu.VMEM((HALF, D), BF),
                pltpu.VMEM((HPC, WIN, WIN), F32),
                pltpu.VMEM((HPC, WIN, WIN), BF),
                pltpu.VMEM((D, 512), BF),
                pltpu.VMEM((512, HALF), BF),
                pltpu.VMEM((HALF, 512), BF),
                pltpu.VMEM((4, HPC, WIN, WIN), F32),
                pltpu.VMEM((512, 3 * HALF), BF),
                pltpu.VMEM((512, 3 * HALF), BF),
                pltpu.SemaphoreType.DMA((72,)),
            ],
            us=21,
        )
    with jax.named_scope("rows_out"):
        owner_rows = lax.all_to_all(outgoing, ("grp", "enc"), split_axis=0, concat_axis=0, tiled=True)
        owner_rows = owner_rows.reshape(512, D)
        owner_rows, terms = lax.optimization_barrier((owner_rows, terms))
    with jax.named_scope("weight_grads"):
        up_a, down_a = scatter_first(*terms[1:3], "x")
        up_b, down_b = scatter_first(*terms[6:8], "z")
    with jax.named_scope("norm_grad"):
        gqkv, up_a, down_a = lax.optimization_barrier((gqkv, up_a, down_a))
        nmine, ntheirs = call(
            norm_grad_kernel,
            [((ROWS, D), F32), ((ROWS, D), BF)],
            (place, gqkv, *part_a, *part_b),
            "sv" + "a" * 10,
            scratch=[pltpu.VMEM((D, 3 * HALF), BF), pltpu.SemaphoreType.DMA((32,))],
            us=8,
        )
    with jax.named_scope("weight_grads"):
        sum_a = scatter_second(terms[0], up_a, down_a, *terms[3:5], "x", "z")
        sum_b = scatter_second(terms[5], up_b, down_b, *terms[8:], "z", "x")
    with jax.named_scope("norm_grad"):
        nfrom = to_sibling(ntheirs)
        (patch_grads,) = call(
            finish_kernel, [((ROWS, D), BF)], (nmine, nfrom, ordered, gain, gown, order_t), "vvvvvv"
        )
    with jax.named_scope("back_to_rows"):
        mine = jnp.concatenate([sum_a, sum_b[:, :HALF]], axis=1).astype(BF)
        low, high = mine[:40], mine[40:]
        got = to_sibling(jnp.where(first_core, high, low))
        keep = jnp.where(first_core, low, high)
        out_terms = sum_b[:, HALF:].astype(BF)
        low, high = out_terms[:40], out_terms[40:]
        out_same = to_halves(jnp.where(x < 2, low, high), True, back=True)
        out_other = to_halves(jnp.where(x < 2, high, low), False, back=True)
        low, high = jnp.where(first_core, keep, got), jnp.where(first_core, got, keep)
        out_low, out_high = jnp.where(first_core, out_same, out_other), jnp.where(first_core, out_other, out_same)
        blocks = jnp.stack(
            [jnp.concatenate([low[:, t * HALF : (t + 1) * HALF], high[:, t * HALF : (t + 1) * HALF]], axis=1) for t in range(3)]
            + [jnp.concatenate([out_low, out_high], axis=1)]
        )
    with jax.named_scope("over_groups"):
        me = lax.axis_index("grp")

        def block(step):
            return lax.dynamic_index_in_dim(blocks, (me + step + 4) % 4, 0, keepdims=False)

        total = block(0).astype(F32)
        for step in STEPS[1:]:
            total = total + hop(block(step), "y", step).astype(F32)
        total = total.astype(BF)
        every = [total] + [hop(total, "y", -step) for step in STEPS[1:]]
        factor = 1.0 / math.sqrt(ROWS * 128)

        def summed(t):
            step = (t - me + 4) % 4
            value = jnp.where(
                step == 0, every[0], jnp.where(step == 1, every[1], jnp.where(step == 3, every[2], every[3]))
            )
            return value.astype(F32) * factor

        qkv_grad = jnp.concatenate([summed(t) for t in range(3)], axis=1)
        out_grad = summed(3)
    return owner_rows, patch_grads, qkv_grad, out_grad


def solution(mesh):
    rows = P(("grp", "enc"), None)
    in_specs = (rows, P(), P("enc", None), P("enc", None), rows, rows, rows, rows)
    out_specs = (rows, rows, P("enc", None), P("enc", None))
    return jax.shard_map(body, mesh=mesh, in_specs=in_specs, out_specs=out_specs, check_vma=False)
```

```python
import math

import jax
import jax.numpy as jnp
from jax import lax
from jax.experimental import pallas as pl
from jax.experimental.pallas import tpu as pltpu
from jax.sharding import PartitionSpec as P

HEADS = 16
HD = 80
WIN = 128
EPSILON = 1e-06
D = 1280
ROWS = 256
HALF = 640
HPC = HEADS // 2
SLOTS = 1024
BF = jnp.bfloat16
F32 = jnp.float32
VMEM_LIMIT = 58 * 1024 * 1024
STEPS = (0, 1, -1, 2)


def ring(axis, step):
    pairs = []
    for x in range(4):
        for z in range(4):
            for c in range(2):
                to = ((x + step) % 4, z) if axis == "x" else (x, (z + step) % 4)
                pairs.append(((x * 4 + z) * 2 + c, (to[0] * 4 + to[1]) * 2 + c))
    return pairs


def hop(value, axis, step):
    if axis == "y":
        return lax.ppermute(value, "grp", [(i, (i + step) % 4) for i in range(4)])
    return lax.ppermute(value, "enc", ring(axis, step))


def to_sibling(value):
    return lax.ppermute(value, "enc", [(i, i ^ 1) for i in range(32)])


def gather_line(shard, first):
    behind = hop(shard, first, 1)
    ahead = hop(shard, first, -1)
    across = hop(shard, first, 2)
    return jnp.stack([shard, ahead, behind, across])


def gather_rest(line, second):
    line_behind = hop(line, second, 1)
    line_ahead = hop(line, second, -1)
    far_low = hop(line_behind[:2], second, 1)
    far_high = hop(line_ahead[2:], second, -1)
    return line, line_ahead, line_behind, far_low, far_high


def add(*values):
    total = values[0].astype(F32)
    for v in values[1:]:
        total = total + v.astype(F32)
    return total


def scatter_first(up, down, axis):
    return hop(up, axis, 1), hop(down, axis, -1)


def scatter_second(own, from_up, from_down, next_up, next_down, first, second):
    last_up = hop(add(next_up, from_up[:2]).astype(BF), first, 1)
    last_down = hop(add(next_down, from_down[:2]).astype(BF), first, -1)
    total = jnp.concatenate([add(own[:2], last_up, from_down[2:]), add(own[2:], from_up[2:], last_down)])
    rounded = total.astype(BF)
    one = hop(rounded[1], second, 1)
    two = hop(rounded[2], second, -1)
    three = hop(rounded[3], second, 2)
    return add(total[0], one, two, three)


def dot(a, b):
    return jnp.dot(a, b, preferred_element_type=F32)


def dot_nt(a, b):
    return lax.dot_general(a, b, (((1,), (1,)), ((), ())), preferred_element_type=F32)


def dot_tn(a, b):
    return lax.dot_general(a, b, (((0,), (0,)), ((), ())), preferred_element_type=F32)


def call(kernel, outs, ins, in_spaces, out_spaces=None, scratch=(), us=3):
    spaces = {"v": pltpu.VMEM, "s": pltpu.SMEM, "a": pltpu.HBM}
    out_spaces = out_spaces or "v" * len(outs)
    return pl.pallas_call(
        kernel,
        out_shape=[jax.ShapeDtypeStruct(s, t) for s, t in outs],
        in_specs=[pl.BlockSpec(memory_space=spaces[c]) for c in in_spaces],
        out_specs=[pl.BlockSpec(memory_space=spaces[c]) for c in out_spaces],
        scratch_shapes=list(scratch),
        compiler_params=pltpu.CompilerParams(vmem_limit_bytes=VMEM_LIMIT),
        cost_estimate=pl.CostEstimate(flops=us * 10**9, bytes_accessed=us * 3 * 10**6, transcendentals=0),
    )(*ins)


def half_of(place, value):
    return jnp.where(place[2] == 0, value[:, :HALF], value[:, HALF:])


def prepare_kernel(place, counts, patches, gain, order, owners, naug, extra, ordered):
    rows = lax.broadcasted_iota(jnp.int32, (ROWS, ROWS), 1)
    perm = (order[...] == rows).astype(BF)
    row = lax.broadcasted_iota(jnp.int32, (ROWS, 128), 0)
    lane = lax.broadcasted_iota(jnp.int32, (ROWS, 128), 1)
    image = jnp.zeros((ROWS, 128), jnp.int32)
    end = 0
    for k in range(4):
        end = end + counts[0, k]
        image = image + (row >= end).astype(jnp.int32)
    kinds = dot(perm, (image == lane).astype(BF)).astype(BF)
    named = (owners[...] == lane).astype(BF)
    earlier = (rows < lax.broadcasted_iota(jnp.int32, (ROWS, ROWS), 0)).astype(BF)
    before = dot(earlier, named)
    slot = jnp.sum(before * named.astype(F32), axis=1, keepdims=True).astype(jnp.int32)
    target = owners[...] * 8 + place[2] * 4 + slot
    slots = lax.broadcasted_iota(jnp.int32, (ROWS, SLOTS), 1)
    extra[:, :SLOTS] = dot(perm, (target == slots).astype(BF)).astype(BF)
    rowsw = dot(perm, patches[...])
    ordered[...] = rowsw.astype(BF)
    extra[:, SLOTS:] = jnp.where(place[2] == 0, rowsw[:, HALF:], rowsw[:, :HALF]).astype(BF)
    spread = lax.rsqrt(jnp.mean(rowsw * rowsw, axis=1, keepdims=True) + EPSILON)
    naug[:, :D] = (rowsw * spread * gain[...]).astype(BF)
    naug[:, D:] = kinds


class Copies:
    def __init__(self, sems):
        self.sems, self.used = sems, 0

    def make(self, src, dst):
        self.used += 1
        return pltpu.make_async_copy(src, dst, self.sems.at[self.used - 1])

    def start(self, src, dst):
        copy = self.make(src, dst)
        copy.start()
        return copy


def wait_all(copies):
    for c in copies:
        c.wait()


def assemble(place, parts, first, copy_one, scatter=False):
    line, ahead, behind, low, high = parts
    x, z = place[0], place[1]
    copies = []
    for i, step in enumerate(STEPS):
        for j, inner in enumerate(STEPS):
            if step == 0:
                ref = line.at[j]
            elif step == 1:
                ref = ahead.at[j]
            elif step == -1:
                ref = behind.at[j]
            else:
                ref = low.at[j] if j < 2 else high.at[j - 2]
            if scatter:
                ref = pieces_at(*parts, step, j)
            if first == "z":
                dx, dz = step, inner
            else:
                dx, dz = inner, step
            copies += copy_one(ref, (x + dx + 4) % 4, (z + dz + 4) % 4)
    return copies


def at_rows(index, size):
    return pl.ds(pl.multiple_of(index * size, size), size)


def take_weights(copies, place, parts, wqkv):
    from_a = assemble(
        place, parts[:5], "z",
        lambda ref, x, z: [copies.start(ref, wqkv.at[at_rows(x * 4 + z, 80), pl.ds(0, 1280)])],
    )
    from_b = assemble(
        place, parts[5:], "x",
        lambda ref, x, z: [
            copies.start(ref.at[:, pl.ds(0, 640)], wqkv.at[at_rows(x * 4 + z, 80), pl.ds(1280, 640)])
        ],
    )
    return from_a, from_b


def take_out(copies, place, parts, wout):
    return assemble(
        place, parts, "x",
        lambda ref, x, z: [copies.start(ref.at[:, pl.ds(640, 640)], wout.at[at_rows(x * 4 + z, 80)])],
    )


def forward_kernel(place, own, sib, a0, a1, a2, a3, a4, b0, b1, b2, b3, b4,
                   probs_out, qkv_out, attended, wqkv, both, scores, probs, qkv, sems):
    copies = Copies(sems)
    from_a, from_b = take_weights(copies, place, (a0, a1, a2, a3, a4, b0, b1, b2, b3, b4), wqkv)
    both[:ROWS, :] = own[:, :D]
    both[ROWS:, :] = sib[:, :D]
    wait_all(from_a)

    def project(col):
        qkv[:, col] = dot(both[...], wqkv[:, col]).astype(BF)

    @pl.loop(0, 5)
    def _(t):
        project(at_rows(t, 256))

    wait_all(from_b)
    project(pl.ds(1280, 256))
    project(pl.ds(1536, 256))
    project(pl.ds(1792, 128))
    out_copies = [copies.start(qkv, qkv_out)]
    scale = HD ** (-0.5)

    @pl.loop(0, 4)
    def _(w):
        rows = at_rows(w, WIN)
        local = at_rows(w % 2, WIN)
        kinds = jnp.where(w < 2, own[local, D:].astype(F32), sib[local, D:].astype(F32)).astype(BF)
        allowed = dot_nt(kinds, kinds) > 0.5
        for h in range(HPC):
            q = qkv[rows, h * HD:(h + 1) * HD]
            k = qkv[rows, HALF + h * HD:HALF + (h + 1) * HD]
            scores[h] = dot_nt(k, q)
        for h in range(HPC):
            s = jnp.where(allowed, scores[h] * scale, -1e30)
            e = jnp.exp(s - jnp.max(s, axis=0, keepdims=True))
            probs[w, h] = e * (1.0 / jnp.sum(e, axis=0, keepdims=True))
        for h in range(HPC):
            v = qkv[rows, 2 * HALF + h * HD:2 * HALF + (h + 1) * HD]
            attended[rows, h * HD:(h + 1) * HD] = dot_tn(probs[w, h].astype(BF), v).astype(BF)

    out_copies.append(copies.start(probs, probs_out))
    wait_all(out_copies)


def embed_kernel(place, attended, other, ordered, extra, sib_extra, b0, b1, b2, b3, b4, out, wout, sems):
    wait_all(take_out(Copies(sems), place, (b0, b1, b2, b3, b4), wout))
    here, there = at_rows(place[2], HALF), at_rows(1 - place[2], HALF)
    mine = dot(attended[:ROWS, :], wout[here, :]) + dot(other[ROWS:, :], wout[there, :])
    theirs = dot(attended[ROWS:, :], wout[here, :]) + dot(other[:ROWS, :], wout[there, :])
    mine = (half_of(place, ordered[...].astype(F32)) + mine).astype(BF)
    theirs = (sib_extra[:, SLOTS:].astype(F32) + theirs).astype(BF)
    total = dot_tn(extra[:, :SLOTS], mine) + dot_tn(sib_extra[:, :SLOTS], theirs)
    out[...] = total.astype(BF)


def pick_kernel(place, returned, extra, sib_extra, b0, b1, b2, b3, b4, grads, mine, theirs, wout, sems):
    copies = take_out(Copies(sems), place, (b0, b1, b2, b3, b4), wout)
    grads[:ROWS, :] = dot(extra[:, :SLOTS], returned[...]).astype(BF)
    grads[ROWS:, :] = dot(sib_extra[:, :SLOTS], returned[...]).astype(BF)
    wait_all(copies)
    mine[...] = dot_nt(grads[...], wout[at_rows(place[2], HALF), :])
    theirs[...] = dot_nt(grads[...], wout[at_rows(1 - place[2], HALF), :]).astype(BF)


def turn_kernel(own, sib, out):
    out[:, :ROWS] = own[:, :D].T
    out[:, ROWS:] = sib[:, :D].T


def pieces_at(own, up, down, next_up, next_down, step, inner):
    if step == 0:
        return own.at[inner]
    if step == 1:
        return next_up.at[inner] if inner < 2 else up.at[inner]
    if step == -1:
        return down.at[inner + 2] if inner < 2 else next_down.at[inner - 2]
    return up.at[inner] if inner < 2 else down.at[inner - 2]


def backward_kernel(place, grads_hbm, ga_mine, ga_other, normed_hbm, probs_hbm, qkv_hbm, attended_hbm, other_hbm,
                    gqkv_out, aown, aup, adown, alow, ahigh, bown, bup, bdown, blow, bhigh,
                    grads, gatt, ga, gb, terms, oterms, scores, small, normed_t, attended, other, attended_t,
                    probs, qkv, gqkv, sems):
    copies = Copies(sems)
    grads_in = [
        copies.start(ga_mine, ga),
        copies.start(ga_other.at[pl.ds(ROWS, ROWS)], gb.at[pl.ds(0, ROWS)]),
        copies.start(ga_other.at[pl.ds(0, ROWS)], gb.at[pl.ds(ROWS, ROWS)]),
    ]
    first_in = [copies.start(qkv_hbm, qkv), copies.start(probs_hbm, probs)]
    second_in = [
        copies.start(attended_hbm, attended),
        copies.start(other_hbm.at[pl.ds(ROWS, ROWS)], other.at[pl.ds(0, ROWS)]),
        copies.start(other_hbm.at[pl.ds(0, ROWS)], other.at[pl.ds(ROWS, ROWS)]),
        copies.start(normed_hbm, normed_t),
        copies.start(grads_hbm, grads),
    ]
    wait_all(grads_in)
    gatt[...] = (ga[...] + gb[...].astype(F32)).astype(BF)
    scale = HD ** (-0.5)
    wait_all(first_in)

    @pl.loop(0, 4)
    def _(w):
        rows = at_rows(w, WIN)
        for h in range(HPC):
            a, b = h * HD, (h + 1) * HD
            scores[h] = dot_nt(qkv[rows, 2 * HALF + a:2 * HALF + b], gatt[rows, a:b])
        for h in range(HPC):
            a, b = h * HD, (h + 1) * HD
            gqkv[rows, 2 * HALF + a:2 * HALF + b] = dot(probs[w, h].astype(BF), gatt[rows, a:b]).astype(BF)
        for h in range(HPC):
            p = probs[w, h]
            g = scores[h]
            inner = jnp.sum(p * g, axis=0, keepdims=True)
            small[h] = (p * (g - inner) * scale).astype(BF)
        for h in range(HPC):
            a, b = h * HD, (h + 1) * HD
            gqkv[rows, HALF + a:HALF + b] = dot(small[h], qkv[rows, a:b]).astype(BF)
            gqkv[rows, a:b] = dot_tn(small[h], qkv[rows, HALF + a:HALF + b]).astype(BF)

    out_copies = [copies.start(gqkv, gqkv_out)]
    wait_all(second_in)

    def weigh(col):
        terms[:, col] = dot(normed_t[...], gqkv[:, col]).astype(BF)

    @pl.loop(0, 5)
    def _(t):
        weigh(at_rows(t, 256))

    out_copies += assemble(
        place, (aown, aup, adown, alow, ahigh), "z",
        lambda ref, x, z: [copies.start(terms.at[at_rows(x * 4 + z, 80), pl.ds(0, 1280)], ref)],
        scatter=True,
    )
    weigh(pl.ds(1280, 256))
    weigh(pl.ds(1536, 256))
    weigh(pl.ds(1792, 128))
    out_copies += assemble(
        place, (bown, bup, bdown, blow, bhigh), "x",
        lambda ref, x, z: [
            copies.start(terms.at[at_rows(x * 4 + z, 80), pl.ds(1280, 640)], ref.at[:, pl.ds(0, 640)])
        ],
        scatter=True,
    )
    attended_t[at_rows(place[2], HALF), :] = attended[...].T
    attended_t[at_rows(1 - place[2], HALF), :] = other[...].T
    for r in range(5):
        rows = slice(r * 256, (r + 1) * 256)
        oterms[rows, :] = dot(attended_t[rows, :], grads[...]).astype(BF)

    out_copies += assemble(
        place, (bown, bup, bdown, blow, bhigh), "x",
        lambda ref, x, z: [copies.start(oterms.at[at_rows(x * 4 + z, 80)], ref.at[:, pl.ds(640, 640)])],
        scatter=True,
    )
    wait_all(out_copies)


def norm_grad_kernel(place, gqkv, a0, a1, a2, a3, a4, b0, b1, b2, b3, b4, mine, theirs, wqkv, sems):
    from_a, from_b = take_weights(Copies(sems), place, (a0, a1, a2, a3, a4, b0, b1, b2, b3, b4), wqkv)
    wait_all(from_a + from_b)
    for t in range(5):
        col = slice(t * 256, (t + 1) * 256)
        part = dot_nt(gqkv[...], wqkv[col, :])
        mine[:, col] = part[:ROWS]
        theirs[:, col] = part[ROWS:].astype(BF)


def finish_kernel(place, mine, theirs, ordered, gain, grads, other, order_t, out):
    rows = lax.broadcasted_iota(jnp.int32, (ROWS, ROWS), 0)
    back = (order_t[...] == rows).astype(BF)
    rowsw = ordered[...].astype(F32)
    spread = lax.rsqrt(jnp.mean(rowsw * rowsw, axis=1, keepdims=True) + EPSILON)
    scaled = rowsw * spread
    normed = (mine[...] + theirs[...].astype(F32)).astype(BF).astype(F32)
    u = normed * gain[...]
    layer = (u - scaled * jnp.mean(u * scaled, axis=1, keepdims=True)) * spread
    here, there = grads[:ROWS, :].astype(F32), other[...].astype(F32)
    first = place[2] == 0
    window = (jnp.where(first, here, there) + layer[:, :HALF]).astype(BF)
    out[:, :HALF] = dot(back, window).astype(BF)
    window = (jnp.where(first, there, here) + layer[:, HALF:]).astype(BF)
    out[:, HALF:] = dot(back, window).astype(BF)


def body(patches, ln_gain, qkv_weight, out_weight, image_counts, window_order, owner_map, owner_grads):
    index = lax.axis_index("enc")
    x, z, core = index // 8, (index // 2) % 4, index % 2
    place = jnp.stack([x, z, core])
    gain = ln_gain.reshape(1, D)
    order = window_order.reshape(ROWS, 1)
    order_t = window_order.reshape(1, ROWS)

    first_core = core == 0
    with jax.named_scope("weights"):

        def columns(half):
            start = half * HALF
            parts = [qkv_weight[:, t * D + start :][:, :HALF] for t in range(3)]
            return jnp.concatenate(parts + [out_weight[:, start : start + HALF]], axis=1)

        low, high = columns(0), columns(1)
        got = to_sibling(jnp.where(first_core, high, low))
        keep = jnp.where(first_core, low, high)
        shard = jnp.where(first_core, jnp.concatenate([keep, got]), jnp.concatenate([got, keep]))
        line_a = gather_line(shard[:, : 2 * HALF], "z")
        line_b = gather_line(shard[:, 2 * HALF :], "x")
        part_a = gather_rest(line_a, "x")
        part_b = gather_rest(line_b, "z")
    with jax.named_scope("prepare"):
        naug, extra, ordered = call(
            prepare_kernel,
            [((ROWS, D + 128), BF), ((ROWS, SLOTS + HALF), BF), ((ROWS, D), BF)],
            (place, image_counts, patches, gain, order, owner_map),
            "ssvvvv",
        )
        nsib, sib_extra = to_sibling(naug), to_sibling(extra)
        (normed_t,) = call(turn_kernel, [((D, 512), BF)], (naug, nsib), "vv")
    with jax.named_scope("grads_in"):
        sent = owner_grads.reshape(64, 8, 2, HALF).transpose(0, 2, 1, 3).reshape(SLOTS, HALF)
        sent, part_a, part_b, normed_t, sib_extra = lax.optimization_barrier((sent, part_a, part_b, normed_t, sib_extra))
        returned = lax.all_to_all(sent, ("grp", "enc"), split_axis=0, concat_axis=0, tiled=True)
    with jax.named_scope("forward"):
        probs, qkv, attended = call(
            forward_kernel,
            [((4, HPC, WIN, WIN), F32), ((512, 3 * HALF), BF), ((512, HALF), BF)],
            (place, naug, nsib, *part_a, *part_b),
            "svv" + "a" * 10,
            "aav",
            scratch=[
                pltpu.VMEM((D, 3 * HALF), BF),
                pltpu.VMEM((512, D), BF),
                pltpu.VMEM((HPC, WIN, WIN), F32),
                pltpu.VMEM((4, HPC, WIN, WIN), F32),
                pltpu.VMEM((512, 3 * HALF), BF),
                pltpu.SemaphoreType.DMA((34,)),
            ],
            us=12,
        )
        other = to_sibling(attended)
        (outgoing,) = call(
            embed_kernel,
            [((SLOTS, HALF), BF)],
            (place, attended, other, ordered, extra, sib_extra, *part_b),
            "svvvvv" + "a" * 5,
            scratch=[pltpu.VMEM((D, HALF), BF), pltpu.SemaphoreType.DMA((16,))],
        )
    with jax.named_scope("grads_in"):
        returned, outgoing = lax.optimization_barrier((returned, outgoing))
        grads, ga_mine, ga_theirs = call(
            pick_kernel,
            [((512, HALF), BF), ((512, HALF), F32), ((512, HALF), BF)],
            (place, returned, extra, sib_extra, *part_b),
            "svvv" + "a" * 5,
            scratch=[pltpu.VMEM((D, HALF), BF), pltpu.SemaphoreType.DMA((16,))],
        )
        ga_other = to_sibling(ga_theirs)
    with jax.named_scope("backward"):
        ga_mine, ga_other, outgoing = lax.optimization_barrier((ga_mine, ga_other, outgoing))
        pieces = [((4, 80, D), BF)] * 3 + [((2, 80, D), BF)] * 2
        gqkv, *terms = call(
            backward_kernel,
            [((512, 3 * HALF), BF)] + pieces + pieces,
            (place, grads, ga_mine, ga_other, normed_t, probs, qkv, attended, other),
            "s" + "a" * 8,
            "a" * 11,
            scratch=[
                pltpu.VMEM((512, HALF), BF),
                pltpu.VMEM((512, HALF), BF),
                pltpu.VMEM((512, HALF), F32),
                pltpu.VMEM((512, HALF), BF),
                pltpu.VMEM((D, 3 * HALF), BF),
                pltpu.VMEM((D, HALF), BF),
                pltpu.VMEM((HPC, WIN, WIN), F32),
                pltpu.VMEM((HPC, WIN, WIN), BF),
                pltpu.VMEM((D, 512), BF),
                pltpu.VMEM((512, HALF), BF),
                pltpu.VMEM((512, HALF), BF),
                pltpu.VMEM((D, 512), BF),
                pltpu.VMEM((4, HPC, WIN, WIN), F32),
                pltpu.VMEM((512, 3 * HALF), BF),
                pltpu.VMEM((512, 3 * HALF), BF),
                pltpu.SemaphoreType.DMA((60,)),
            ],
            us=21,
        )
    with jax.named_scope("rows_out"):
        owner_rows = lax.all_to_all(outgoing, ("grp", "enc"), split_axis=0, concat_axis=0, tiled=True)
        owner_rows, terms = lax.optimization_barrier((owner_rows, terms))
        owner_rows = owner_rows.reshape(64, 2, 8, HALF).transpose(0, 2, 1, 3).reshape(512, D)
    with jax.named_scope("weight_grads"):
        up_a, down_a = scatter_first(*terms[1:3], "x")
        up_b, down_b = scatter_first(*terms[6:8], "z")
    with jax.named_scope("norm_grad"):
        tick = hop(terms[1][0, :16, :128], "y", 1)
        gqkv, tick = lax.optimization_barrier((gqkv, tick))
        nmine, ntheirs = call(
            norm_grad_kernel,
            [((ROWS, D), F32), ((ROWS, D), BF)],
            (place, gqkv, *part_a, *part_b),
            "sv" + "a" * 10,
            scratch=[pltpu.VMEM((D, 3 * HALF), BF), pltpu.SemaphoreType.DMA((32,))],
            us=8,
        )
    with jax.named_scope("weight_grads"):
        up_a, down_a, up_b, down_b, ntheirs = lax.optimization_barrier((up_a, down_a, up_b, down_b, ntheirs))
        sum_a = scatter_second(terms[0], up_a, down_a, *terms[3:5], "x", "z")
        sum_b = scatter_second(terms[5], up_b, down_b, *terms[8:], "z", "x")
    with jax.named_scope("norm_grad"):
        nfrom = to_sibling(ntheirs)
        grads_other = to_sibling(grads[ROWS:])
        (patch_grads,) = call(
            finish_kernel,
            [((ROWS, D), BF)],
            (place, nmine, nfrom, ordered, gain, grads, grads_other, order_t),
            "svvvvvvv",
        )
    with jax.named_scope("back_to_rows"):
        mine = jnp.concatenate([sum_a, sum_b], axis=1).astype(BF)
        low, high = mine[:40], mine[40:]
        got = to_sibling(jnp.where(first_core, high, low))
        keep = jnp.where(first_core, low, high)
        low, high = jnp.where(first_core, keep, got), jnp.where(first_core, got, keep)
        blocks = jnp.stack(
            [jnp.concatenate([low[:, t * HALF : (t + 1) * HALF], high[:, t * HALF : (t + 1) * HALF]], axis=1) for t in range(4)]
        )
    with jax.named_scope("over_groups"):
        me = lax.axis_index("grp")

        def block(step):
            return lax.dynamic_index_in_dim(blocks, (me + step + 4) % 4, 0, keepdims=False)

        total = block(0).astype(F32)
        for step in STEPS[1:]:
            total = total + hop(block(step), "y", step).astype(F32)
        total = total.astype(BF)
        every = [total] + [hop(total, "y", -step) for step in STEPS[1:]]
        factor = 1.0 / math.sqrt(ROWS * 128)

        def summed(t):
            step = (t - me + 4) % 4
            value = jnp.where(
                step == 0, every[0], jnp.where(step == 1, every[1], jnp.where(step == 3, every[2], every[3]))
            )
            return value.astype(F32) * factor

        qkv_grad = jnp.concatenate([summed(t) for t in range(3)], axis=1)
        out_grad = summed(3)
    return owner_rows, patch_grads, qkv_grad, out_grad


def solution(mesh):
    rows = P(("grp", "enc"), None)
    in_specs = (rows, P(), P("enc", None), P("enc", None), rows, rows, rows, rows)
    out_specs = (rows, rows, P("enc", None), P("enc", None))
    return jax.shard_map(body, mesh=mesh, in_specs=in_specs, out_specs=out_specs, check_vma=False)
```

```python
import math

import jax
import jax.numpy as jnp
from jax import lax
from jax.experimental import pallas as pl
from jax.experimental.pallas import tpu as pltpu
from jax.sharding import PartitionSpec as P

HEADS = 16
HD = 80
WIN = 128
EPSILON = 1e-06
D = 1280
ROWS = 256
HALF = 640
HPC = HEADS // 2
SLOTS = 1024
BF = jnp.bfloat16
F32 = jnp.float32
VMEM_LIMIT = 58 * 1024 * 1024
STEPS = (0, 1, -1, 2)


def ring(axis, step):
    pairs = []
    for x in range(4):
        for z in range(4):
            for c in range(2):
                to = ((x + step) % 4, z) if axis == "x" else (x, (z + step) % 4)
                pairs.append(((x * 4 + z) * 2 + c, (to[0] * 4 + to[1]) * 2 + c))
    return pairs


def hop(value, axis, step):
    if axis == "y":
        return lax.ppermute(value, "grp", [(i, (i + step) % 4) for i in range(4)])
    return lax.ppermute(value, "enc", ring(axis, step))


def to_sibling(value):
    return lax.ppermute(value, "enc", [(i, i ^ 1) for i in range(32)])


def gather_line(shard, first):
    behind = hop(shard, first, 1)
    ahead = hop(shard, first, -1)
    across = hop(shard, first, 2)
    return jnp.stack([shard, ahead, behind, across])


def gather_rest(line, second):
    line_behind = hop(line, second, 1)
    line_ahead = hop(line, second, -1)
    far_low = hop(line_behind[:2], second, 1)
    far_high = hop(line_ahead[2:], second, -1)
    return line, line_ahead, line_behind, far_low, far_high


def add(*values):
    total = values[0].astype(F32)
    for v in values[1:]:
        total = total + v.astype(F32)
    return total


def scatter_first(up, down, axis):
    return hop(up, axis, 1), hop(down, axis, -1)


def scatter_second(own, from_up, from_down, next_up, next_down, first, second):
    last_up = hop(add(next_up, from_up[:2]).astype(BF), first, 1)
    last_down = hop(add(next_down, from_down[:2]).astype(BF), first, -1)
    total = jnp.concatenate([add(own[:2], last_up, from_down[2:]), add(own[2:], from_up[2:], last_down)])
    rounded = total.astype(BF)
    one = hop(rounded[1], second, 1)
    two = hop(rounded[2], second, -1)
    three = hop(rounded[3], second, 2)
    return add(total[0], one, two, three)


def dot(a, b):
    return jnp.dot(a, b, preferred_element_type=F32)


def dot_nt(a, b):
    return lax.dot_general(a, b, (((1,), (1,)), ((), ())), preferred_element_type=F32)


def dot_tn(a, b):
    return lax.dot_general(a, b, (((0,), (0,)), ((), ())), preferred_element_type=F32)


def call(kernel, outs, ins, in_spaces, out_spaces=None, scratch=(), us=3):
    spaces = {"v": pltpu.VMEM, "s": pltpu.SMEM, "a": pltpu.HBM}
    out_spaces = out_spaces or "v" * len(outs)
    return pl.pallas_call(
        kernel,
        out_shape=[jax.ShapeDtypeStruct(s, t) for s, t in outs],
        in_specs=[pl.BlockSpec(memory_space=spaces[c]) for c in in_spaces],
        out_specs=[pl.BlockSpec(memory_space=spaces[c]) for c in out_spaces],
        scratch_shapes=list(scratch),
        compiler_params=pltpu.CompilerParams(vmem_limit_bytes=VMEM_LIMIT),
        cost_estimate=pl.CostEstimate(flops=us * 10**9, bytes_accessed=us * 3 * 10**6, transcendentals=0),
    )(*ins)


def half_of(place, value):
    return jnp.where(place[2] == 0, value[:, :HALF], value[:, HALF:])


def prepare_kernel(place, counts, patches, gain, order, owners, naug, extra, ordered):
    rows = lax.broadcasted_iota(jnp.int32, (ROWS, ROWS), 1)
    perm = (order[...] == rows).astype(BF)
    row = lax.broadcasted_iota(jnp.int32, (ROWS, 128), 0)
    lane = lax.broadcasted_iota(jnp.int32, (ROWS, 128), 1)
    image = jnp.zeros((ROWS, 128), jnp.int32)
    end = 0
    for k in range(4):
        end = end + counts[0, k]
        image = image + (row >= end).astype(jnp.int32)
    kinds = dot(perm, (image == lane).astype(BF)).astype(BF)
    named = (owners[...] == lane).astype(BF)
    earlier = (rows < lax.broadcasted_iota(jnp.int32, (ROWS, ROWS), 0)).astype(BF)
    before = dot(earlier, named)
    slot = jnp.sum(before * named.astype(F32), axis=1, keepdims=True).astype(jnp.int32)
    target = owners[...] * 8 + place[2] * 4 + slot
    slots = lax.broadcasted_iota(jnp.int32, (ROWS, SLOTS), 1)
    extra[:, :SLOTS] = dot(perm, (target == slots).astype(BF)).astype(BF)
    rowsw = dot(perm, patches[...])
    ordered[...] = rowsw.astype(BF)
    extra[:, SLOTS:] = jnp.where(place[2] == 0, rowsw[:, HALF:], rowsw[:, :HALF]).astype(BF)
    spread = lax.rsqrt(jnp.mean(rowsw * rowsw, axis=1, keepdims=True) + EPSILON)
    naug[:, :D] = (rowsw * spread * gain[...]).astype(BF)
    naug[:, D:] = kinds


class Copies:
    def __init__(self, sems):
        self.sems, self.used = sems, 0

    def make(self, src, dst):
        self.used += 1
        return pltpu.make_async_copy(src, dst, self.sems.at[self.used - 1])

    def start(self, src, dst):
        copy = self.make(src, dst)
        copy.start()
        return copy


def wait_all(copies):
    for c in copies:
        c.wait()


def assemble(place, parts, first, copy_one, scatter=False):
    line, ahead, behind, low, high = parts
    x, z = place[0], place[1]
    copies = []
    for i, step in enumerate(STEPS):
        for j, inner in enumerate(STEPS):
            if step == 0:
                ref = line.at[j]
            elif step == 1:
                ref = ahead.at[j]
            elif step == -1:
                ref = behind.at[j]
            else:
                ref = low.at[j] if j < 2 else high.at[j - 2]
            if scatter:
                ref = pieces_at(*parts, step, j)
            if first == "z":
                dx, dz = step, inner
            else:
                dx, dz = inner, step
            copies += copy_one(ref, (x + dx + 4) % 4, (z + dz + 4) % 4)
    return copies


def at_rows(index, size):
    return pl.ds(pl.multiple_of(index * size, size), size)


def take_weights(copies, place, parts, wqkv):
    from_a = assemble(
        place, parts[:5], "z",
        lambda ref, x, z: [copies.start(ref, wqkv.at[at_rows(x * 4 + z, 80), pl.ds(0, 1280)])],
    )
    from_b = assemble(
        place, parts[5:], "x",
        lambda ref, x, z: [
            copies.start(ref.at[:, pl.ds(0, 640)], wqkv.at[at_rows(x * 4 + z, 80), pl.ds(1280, 640)])
        ],
    )
    return from_a, from_b


def take_out(copies, place, parts, wout):
    return assemble(
        place, parts, "x",
        lambda ref, x, z: [copies.start(ref.at[:, pl.ds(640, 640)], wout.at[at_rows(x * 4 + z, 80)])],
    )


def forward_kernel(place, own, sib, a0, a1, a2, a3, a4, b0, b1, b2, b3, b4,
                   probs_out, qkv_out, attended, wqkv, both, scores, probs, qkv, sems):
    copies = Copies(sems)
    from_a, from_b = take_weights(copies, place, (a0, a1, a2, a3, a4, b0, b1, b2, b3, b4), wqkv)
    both[:ROWS, :] = own[:, :D]
    both[ROWS:, :] = sib[:, :D]
    wait_all(from_a)

    def project(col):
        qkv[:, col] = dot(both[...], wqkv[:, col]).astype(BF)

    @pl.loop(0, 5)
    def _(t):
        project(at_rows(t, 256))

    wait_all(from_b)
    project(pl.ds(1280, 256))
    project(pl.ds(1536, 256))
    project(pl.ds(1792, 128))
    out_copies = [copies.start(qkv, qkv_out)]
    scale = HD ** (-0.5)

    @pl.loop(0, 4)
    def _(w):
        rows = at_rows(w, WIN)
        local = at_rows(w % 2, WIN)
        kinds = jnp.where(w < 2, own[local, D:].astype(F32), sib[local, D:].astype(F32)).astype(BF)
        allowed = dot_nt(kinds, kinds) > 0.5
        outs = []
        for group in range(0, HPC, 8):
            heads = [(h, h * HD, (h + 1) * HD) for h in range(group, group + 8)]
            for h, a, b in heads:
                scores[h] = dot_nt(qkv[rows, HALF + a:HALF + b], qkv[rows, a:b])
            for h, a, b in heads:
                s = jnp.where(allowed, scores[h] * scale, -1e30)
                e = jnp.exp(s - jnp.max(s, axis=0, keepdims=True))
                probs[w, h] = e * (1.0 / jnp.sum(e, axis=0, keepdims=True))
            for h, a, b in heads:
                outs.append(dot_tn(probs[w, h].astype(BF), qkv[rows, 2 * HALF + a:2 * HALF + b]).astype(BF))
        attended[rows, :] = jnp.concatenate(outs, axis=1)

    out_copies.append(copies.start(probs, probs_out))
    wait_all(out_copies)


def embed_kernel(place, attended, other, ordered, extra, sib_extra, b0, b1, b2, b3, b4, out, wout, sems):
    wait_all(take_out(Copies(sems), place, (b0, b1, b2, b3, b4), wout))
    here, there = at_rows(place[2], HALF), at_rows(1 - place[2], HALF)
    mine = dot(attended[:ROWS, :], wout[here, :]) + dot(other[ROWS:, :], wout[there, :])
    theirs = dot(attended[ROWS:, :], wout[here, :]) + dot(other[:ROWS, :], wout[there, :])
    mine = (half_of(place, ordered[...].astype(F32)) + mine).astype(BF)
    theirs = (sib_extra[:, SLOTS:].astype(F32) + theirs).astype(BF)
    total = dot_tn(extra[:, :SLOTS], mine) + dot_tn(sib_extra[:, :SLOTS], theirs)
    out[...] = total.astype(BF)


def pick_kernel(place, returned, extra, sib_extra, b0, b1, b2, b3, b4, grads, mine, theirs, wout, sems):
    copies = take_out(Copies(sems), place, (b0, b1, b2, b3, b4), wout)
    grads[:ROWS, :] = dot(extra[:, :SLOTS], returned[...]).astype(BF)
    grads[ROWS:, :] = dot(sib_extra[:, :SLOTS], returned[...]).astype(BF)
    wait_all(copies)
    mine[...] = dot_nt(grads[...], wout[at_rows(place[2], HALF), :])
    theirs[...] = dot_nt(grads[...], wout[at_rows(1 - place[2], HALF), :]).astype(BF)


def turn_kernel(own, sib, out):
    out[:, :ROWS] = own[:, :D].T
    out[:, ROWS:] = sib[:, :D].T


def pieces_at(own, up, down, next_up, next_down, step, inner):
    if step == 0:
        return own.at[inner]
    if step == 1:
        return next_up.at[inner] if inner < 2 else up.at[inner]
    if step == -1:
        return down.at[inner + 2] if inner < 2 else next_down.at[inner - 2]
    return up.at[inner] if inner < 2 else down.at[inner - 2]


def backward_kernel(place, grads_hbm, ga_mine, ga_other, normed_hbm, probs_hbm, qkv_hbm, attended_hbm, other_hbm,
                    gqkv_out, aown, aup, adown, alow, ahigh, bown, bup, bdown, blow, bhigh,
                    grads, gatt, ga, gb, terms, oterms, scores, small, normed_t, attended, other, attended_t,
                    probs, qkv, gqkv, sems):
    copies = Copies(sems)
    grads_in = [
        copies.start(ga_mine, ga),
        copies.start(ga_other.at[pl.ds(ROWS, ROWS)], gb.at[pl.ds(0, ROWS)]),
        copies.start(ga_other.at[pl.ds(0, ROWS)], gb.at[pl.ds(ROWS, ROWS)]),
    ]
    first_in = [copies.start(qkv_hbm, qkv), copies.start(probs_hbm, probs)]
    second_in = [
        copies.start(attended_hbm, attended),
        copies.start(other_hbm.at[pl.ds(ROWS, ROWS)], other.at[pl.ds(0, ROWS)]),
        copies.start(other_hbm.at[pl.ds(0, ROWS)], other.at[pl.ds(ROWS, ROWS)]),
        copies.start(normed_hbm, normed_t),
        copies.start(grads_hbm, grads),
    ]
    wait_all(grads_in)
    gatt[...] = (ga[...] + gb[...].astype(F32)).astype(BF)
    scale = HD ** (-0.5)
    wait_all(first_in)

    @pl.loop(0, 4)
    def _(w):
        rows = at_rows(w, WIN)
        to_query, to_key, to_value = [], [], []
        for group in range(0, HPC, 8):
            heads = [(h, h * HD, (h + 1) * HD) for h in range(group, group + 8)]
            for h, a, b in heads:
                scores[h] = dot_nt(qkv[rows, 2 * HALF + a:2 * HALF + b], gatt[rows, a:b])
            for h, a, b in heads:
                to_value.append(dot(probs[w, h].astype(BF), gatt[rows, a:b]).astype(BF))
            for h, a, b in heads:
                p = probs[w, h]
                g = scores[h]
                inner = jnp.sum(p * g, axis=0, keepdims=True)
                small[h] = (p * (g - inner) * scale).astype(BF)
            for h, a, b in heads:
                to_key.append(dot(small[h], qkv[rows, a:b]).astype(BF))
                to_query.append(dot_tn(small[h], qkv[rows, HALF + a:HALF + b]).astype(BF))
        gqkv[rows, :HALF] = jnp.concatenate(to_query, axis=1)
        gqkv[rows, HALF:2 * HALF] = jnp.concatenate(to_key, axis=1)
        gqkv[rows, 2 * HALF:] = jnp.concatenate(to_value, axis=1)

    out_copies = [copies.start(gqkv, gqkv_out)]
    wait_all(second_in)

    def weigh(col):
        terms[:, col] = dot(normed_t[...], gqkv[:, col]).astype(BF)

    @pl.loop(0, 5)
    def _(t):
        weigh(at_rows(t, 256))

    out_copies += assemble(
        place, (aown, aup, adown, alow, ahigh), "z",
        lambda ref, x, z: [copies.start(terms.at[at_rows(x * 4 + z, 80), pl.ds(0, 1280)], ref)],
        scatter=True,
    )
    weigh(pl.ds(1280, 256))
    weigh(pl.ds(1536, 256))
    weigh(pl.ds(1792, 128))
    out_copies += assemble(
        place, (bown, bup, bdown, blow, bhigh), "x",
        lambda ref, x, z: [
            copies.start(terms.at[at_rows(x * 4 + z, 80), pl.ds(1280, 640)], ref.at[:, pl.ds(0, 640)])
        ],
        scatter=True,
    )
    attended_t[at_rows(place[2], HALF), :] = attended[...].T
    attended_t[at_rows(1 - place[2], HALF), :] = other[...].T
    for r in range(5):
        rows = slice(r * 256, (r + 1) * 256)
        oterms[rows, :] = dot(attended_t[rows, :], grads[...]).astype(BF)

    out_copies += assemble(
        place, (bown, bup, bdown, blow, bhigh), "x",
        lambda ref, x, z: [copies.start(oterms.at[at_rows(x * 4 + z, 80)], ref.at[:, pl.ds(640, 640)])],
        scatter=True,
    )
    wait_all(out_copies)


def norm_grad_kernel(place, gqkv, a0, a1, a2, a3, a4, b0, b1, b2, b3, b4, mine, theirs, wqkv, sems):
    from_a, from_b = take_weights(Copies(sems), place, (a0, a1, a2, a3, a4, b0, b1, b2, b3, b4), wqkv)
    wait_all(from_a + from_b)
    for t in range(5):
        col = slice(t * 256, (t + 1) * 256)
        part = dot_nt(gqkv[...], wqkv[col, :])
        mine[:, col] = part[:ROWS]
        theirs[:, col] = part[ROWS:].astype(BF)


def finish_kernel(place, mine, theirs, ordered, gain, grads, other, order_t, out):
    rows = lax.broadcasted_iota(jnp.int32, (ROWS, ROWS), 0)
    back = (order_t[...] == rows).astype(BF)
    rowsw = ordered[...].astype(F32)
    spread = lax.rsqrt(jnp.mean(rowsw * rowsw, axis=1, keepdims=True) + EPSILON)
    scaled = rowsw * spread
    normed = (mine[...] + theirs[...].astype(F32)).astype(BF).astype(F32)
    u = normed * gain[...]
    layer = (u - scaled * jnp.mean(u * scaled, axis=1, keepdims=True)) * spread
    here, there = grads[:ROWS, :].astype(F32), other[...].astype(F32)
    first = place[2] == 0
    window = (jnp.where(first, here, there) + layer[:, :HALF]).astype(BF)
    out[:, :HALF] = dot(back, window).astype(BF)
    window = (jnp.where(first, there, here) + layer[:, HALF:]).astype(BF)
    out[:, HALF:] = dot(back, window).astype(BF)


def body(patches, ln_gain, qkv_weight, out_weight, image_counts, window_order, owner_map, owner_grads):
    index = lax.axis_index("enc")
    x, z, core = index // 8, (index // 2) % 4, index % 2
    place = jnp.stack([x, z, core])
    gain = ln_gain.reshape(1, D)
    order = window_order.reshape(ROWS, 1)
    order_t = window_order.reshape(1, ROWS)

    first_core = core == 0
    with jax.named_scope("weights"):

        def columns(half):
            start = half * HALF
            parts = [qkv_weight[:, t * D + start :][:, :HALF] for t in range(3)]
            return jnp.concatenate(parts + [out_weight[:, start : start + HALF]], axis=1)

        low, high = columns(0), columns(1)
        got = to_sibling(jnp.where(first_core, high, low))
        keep = jnp.where(first_core, low, high)
        shard = jnp.where(first_core, jnp.concatenate([keep, got]), jnp.concatenate([got, keep]))
        line_a = gather_line(shard[:, : 2 * HALF], "z")
        line_b = gather_line(shard[:, 2 * HALF :], "x")
        part_a = gather_rest(line_a, "x")
        part_b = gather_rest(line_b, "z")
    with jax.named_scope("prepare"):
        naug, extra, ordered = call(
            prepare_kernel,
            [((ROWS, D + 128), BF), ((ROWS, SLOTS + HALF), BF), ((ROWS, D), BF)],
            (place, image_counts, patches, gain, order, owner_map),
            "ssvvvv",
        )
        nsib, sib_extra = to_sibling(naug), to_sibling(extra)
        (normed_t,) = call(turn_kernel, [((D, 512), BF)], (naug, nsib), "vv")
    with jax.named_scope("grads_in"):
        sent = owner_grads.reshape(64, 8, 2, HALF).transpose(0, 2, 1, 3).reshape(SLOTS, HALF)
        sent, part_a, part_b, normed_t, sib_extra = lax.optimization_barrier((sent, part_a, part_b, normed_t, sib_extra))
        returned = lax.all_to_all(sent, ("grp", "enc"), split_axis=0, concat_axis=0, tiled=True)
    with jax.named_scope("forward"):
        probs, qkv, attended = call(
            forward_kernel,
            [((4, HPC, WIN, WIN), F32), ((512, 3 * HALF), BF), ((512, HALF), BF)],
            (place, naug, nsib, *part_a, *part_b),
            "svv" + "a" * 10,
            "aav",
            scratch=[
                pltpu.VMEM((D, 3 * HALF), BF),
                pltpu.VMEM((512, D), BF),
                pltpu.VMEM((HPC, WIN, WIN), F32),
                pltpu.VMEM((4, HPC, WIN, WIN), F32),
                pltpu.VMEM((512, 3 * HALF), BF),
                pltpu.SemaphoreType.DMA((34,)),
            ],
            us=12,
        )
        other = to_sibling(attended)
        (outgoing,) = call(
            embed_kernel,
            [((SLOTS, HALF), BF)],
            (place, attended, other, ordered, extra, sib_extra, *part_b),
            "svvvvv" + "a" * 5,
            scratch=[pltpu.VMEM((D, HALF), BF), pltpu.SemaphoreType.DMA((16,))],
        )
    with jax.named_scope("grads_in"):
        returned, outgoing = lax.optimization_barrier((returned, outgoing))
        grads, ga_mine, ga_theirs = call(
            pick_kernel,
            [((512, HALF), BF), ((512, HALF), F32), ((512, HALF), BF)],
            (place, returned, extra, sib_extra, *part_b),
            "svvv" + "a" * 5,
            scratch=[pltpu.VMEM((D, HALF), BF), pltpu.SemaphoreType.DMA((16,))],
        )
        ga_mine, ga_theirs, outgoing = lax.optimization_barrier((ga_mine, ga_theirs, outgoing))
        ga_other = to_sibling(ga_theirs)
    with jax.named_scope("backward"):
        pieces = [((4, 80, D), BF)] * 3 + [((2, 80, D), BF)] * 2
        gqkv, *terms = call(
            backward_kernel,
            [((512, 3 * HALF), BF)] + pieces + pieces,
            (place, grads, ga_mine, ga_other, normed_t, probs, qkv, attended, other),
            "s" + "a" * 8,
            "a" * 11,
            scratch=[
                pltpu.VMEM((512, HALF), BF),
                pltpu.VMEM((512, HALF), BF),
                pltpu.VMEM((512, HALF), F32),
                pltpu.VMEM((512, HALF), BF),
                pltpu.VMEM((D, 3 * HALF), BF),
                pltpu.VMEM((D, HALF), BF),
                pltpu.VMEM((HPC, WIN, WIN), F32),
                pltpu.VMEM((HPC, WIN, WIN), BF),
                pltpu.VMEM((D, 512), BF),
                pltpu.VMEM((512, HALF), BF),
                pltpu.VMEM((512, HALF), BF),
                pltpu.VMEM((D, 512), BF),
                pltpu.VMEM((4, HPC, WIN, WIN), F32),
                pltpu.VMEM((512, 3 * HALF), BF),
                pltpu.VMEM((512, 3 * HALF), BF),
                pltpu.SemaphoreType.DMA((60,)),
            ],
            us=1,
        )
    with jax.named_scope("rows_out"):
        owner_rows = lax.all_to_all(outgoing, ("grp", "enc"), split_axis=0, concat_axis=0, tiled=True)
        owner_rows = owner_rows.reshape(64, 2, 8, HALF).transpose(0, 2, 1, 3).reshape(512, D)
    with jax.named_scope("weight_grads"):
        up_a, down_a = scatter_first(*terms[1:3], "x")
        up_b, down_b = scatter_first(*terms[6:8], "z")
    with jax.named_scope("norm_grad"):
        tick = hop(terms[1][0, :16, :128], "y", 1)
        gqkv, tick = lax.optimization_barrier((gqkv, tick))
        nmine, ntheirs = call(
            norm_grad_kernel,
            [((ROWS, D), F32), ((ROWS, D), BF)],
            (place, gqkv, *part_a, *part_b),
            "sv" + "a" * 10,
            scratch=[pltpu.VMEM((D, 3 * HALF), BF), pltpu.SemaphoreType.DMA((32,))],
            us=1,
        )
    with jax.named_scope("weight_grads"):
        up_a, down_a, up_b, down_b, ntheirs, owner_rows = lax.optimization_barrier(
            (up_a, down_a, up_b, down_b, ntheirs, owner_rows)
        )
        sum_a = scatter_second(terms[0], up_a, down_a, *terms[3:5], "x", "z")
        sum_b = scatter_second(terms[5], up_b, down_b, *terms[8:], "z", "x")
    with jax.named_scope("norm_grad"):
        nfrom = to_sibling(ntheirs)
        grads_other = to_sibling(grads[ROWS:])
        (patch_grads,) = call(
            finish_kernel,
            [((ROWS, D), BF)],
            (place, nmine, nfrom, ordered, gain, grads, grads_other, order_t),
            "svvvvvvv",
        )
    with jax.named_scope("back_to_rows"):
        mine = jnp.concatenate([sum_a, sum_b], axis=1).astype(BF)
        low, high = mine[:40], mine[40:]
        got = to_sibling(jnp.where(first_core, high, low))
        keep = jnp.where(first_core, low, high)
        low, high = jnp.where(first_core, keep, got), jnp.where(first_core, got, keep)
        blocks = jnp.stack(
            [jnp.concatenate([low[:, t * HALF : (t + 1) * HALF], high[:, t * HALF : (t + 1) * HALF]], axis=1) for t in range(4)]
        )
    with jax.named_scope("over_groups"):
        me = lax.axis_index("grp")

        def block(step):
            return lax.dynamic_index_in_dim(blocks, (me + step + 4) % 4, 0, keepdims=False)

        total = block(0).astype(F32)
        for step in STEPS[1:]:
            total = total + hop(block(step), "y", step).astype(F32)
        total = total.astype(BF)
        every = [total] + [hop(total, "y", -step) for step in STEPS[1:]]
        factor = 1.0 / math.sqrt(ROWS * 128)

        def summed(t):
            step = (t - me + 4) % 4
            value = jnp.where(
                step == 0, every[0], jnp.where(step == 1, every[1], jnp.where(step == 3, every[2], every[3]))
            )
            return value.astype(F32) * factor

        qkv_grad = jnp.concatenate([summed(t) for t in range(3)], axis=1)
        out_grad = summed(3)
    return owner_rows, patch_grads, qkv_grad, out_grad


def solution(mesh):
    rows = P(("grp", "enc"), None)
    in_specs = (rows, P(), P("enc", None), P("enc", None), rows, rows, rows, rows)
    out_specs = (rows, rows, P("enc", None), P("enc", None))
    return jax.shard_map(body, mesh=mesh, in_specs=in_specs, out_specs=out_specs, check_vma=False)
```

```python
import math

import jax
import jax.numpy as jnp
from jax import lax
from jax.experimental import pallas as pl
from jax.experimental.pallas import tpu as pltpu
from jax.sharding import PartitionSpec as P

HEADS = 16
HD = 80
WIN = 128
EPSILON = 1e-06
D = 1280
ROWS = 256
HALF = 640
HPC = HEADS // 2
SLOTS = 1024
BF = jnp.bfloat16
F32 = jnp.float32
VMEM_LIMIT = 58 * 1024 * 1024
STEPS = (0, 1, -1, 2)


def ring(axis, step):
    pairs = []
    for x in range(4):
        for z in range(4):
            for c in range(2):
                to = ((x + step) % 4, z) if axis == "x" else (x, (z + step) % 4)
                pairs.append(((x * 4 + z) * 2 + c, (to[0] * 4 + to[1]) * 2 + c))
    return pairs


def hop(value, axis, step):
    if axis == "y":
        return lax.ppermute(value, "grp", [(i, (i + step) % 4) for i in range(4)])
    return lax.ppermute(value, "enc", ring(axis, step))


def to_sibling(value):
    return lax.ppermute(value, "enc", [(i, i ^ 1) for i in range(32)])


def gather_line(shard, first):
    behind = hop(shard, first, 1)
    ahead = hop(shard, first, -1)
    across = hop(shard, first, 2)
    return jnp.stack([shard, ahead, behind, across])


def gather_rest(line, second):
    line_behind = hop(line, second, 1)
    line_ahead = hop(line, second, -1)
    far_low = hop(line_behind[:2], second, 1)
    far_high = hop(line_ahead[2:], second, -1)
    return line, line_ahead, line_behind, far_low, far_high


def add(*values):
    total = values[0].astype(F32)
    for v in values[1:]:
        total = total + v.astype(F32)
    return total


def scatter_first(up, down, axis):
    return hop(up, axis, 1), hop(down, axis, -1)


def scatter_second(own, from_up, from_down, next_up, next_down, first, second):
    last_up = hop(add(next_up, from_up[:2]).astype(BF), first, 1)
    last_down = hop(add(next_down, from_down[:2]).astype(BF), first, -1)
    total = jnp.concatenate([add(own[:2], last_up, from_down[2:]), add(own[2:], from_up[2:], last_down)])
    rounded = total.astype(BF)
    one = hop(rounded[1], second, 1)
    two = hop(rounded[2], second, -1)
    three = hop(rounded[3], second, 2)
    return add(total[0], one, two, three)


def dot(a, b):
    return jnp.dot(a, b, preferred_element_type=F32)


def dot_nt(a, b):
    return lax.dot_general(a, b, (((1,), (1,)), ((), ())), preferred_element_type=F32)


def dot_tn(a, b):
    return lax.dot_general(a, b, (((0,), (0,)), ((), ())), preferred_element_type=F32)


def call(kernel, outs, ins, in_spaces, out_spaces=None, scratch=(), us=3):
    spaces = {"v": pltpu.VMEM, "s": pltpu.SMEM, "a": pltpu.HBM}
    out_spaces = out_spaces or "v" * len(outs)
    return pl.pallas_call(
        kernel,
        out_shape=[jax.ShapeDtypeStruct(s, t) for s, t in outs],
        in_specs=[pl.BlockSpec(memory_space=spaces[c]) for c in in_spaces],
        out_specs=[pl.BlockSpec(memory_space=spaces[c]) for c in out_spaces],
        scratch_shapes=list(scratch),
        compiler_params=pltpu.CompilerParams(vmem_limit_bytes=VMEM_LIMIT),
        cost_estimate=pl.CostEstimate(flops=us * 10**9, bytes_accessed=us * 3 * 10**6, transcendentals=0),
    )(*ins)


def half_of(place, value):
    return jnp.where(place[2] == 0, value[:, :HALF], value[:, HALF:])


def prepare_kernel(place, counts, patches, gain, order, owners, naug, extra, ordered):
    rows = lax.broadcasted_iota(jnp.int32, (ROWS, ROWS), 1)
    perm = (order[...] == rows).astype(BF)
    row = lax.broadcasted_iota(jnp.int32, (ROWS, 128), 0)
    lane = lax.broadcasted_iota(jnp.int32, (ROWS, 128), 1)
    image = jnp.zeros((ROWS, 128), jnp.int32)
    end = 0
    for k in range(4):
        end = end + counts[0, k]
        image = image + (row >= end).astype(jnp.int32)
    kinds = dot(perm, (image == lane).astype(BF)).astype(BF)
    named = (owners[...] == lane).astype(BF)
    earlier = (rows < lax.broadcasted_iota(jnp.int32, (ROWS, ROWS), 0)).astype(BF)
    before = dot(earlier, named)
    slot = jnp.sum(before * named.astype(F32), axis=1, keepdims=True).astype(jnp.int32)
    target = owners[...] * 8 + place[2] * 4 + slot
    slots = lax.broadcasted_iota(jnp.int32, (ROWS, SLOTS), 1)
    extra[:, :SLOTS] = dot(perm, (target == slots).astype(BF)).astype(BF)
    rowsw = dot(perm, patches[...])
    ordered[...] = rowsw.astype(BF)
    extra[:, SLOTS:] = jnp.where(place[2] == 0, rowsw[:, HALF:], rowsw[:, :HALF]).astype(BF)
    spread = lax.rsqrt(jnp.mean(rowsw * rowsw, axis=1, keepdims=True) + EPSILON)
    naug[:, :D] = (rowsw * spread * gain[...]).astype(BF)
    naug[:, D:] = kinds


class Copies:
    def __init__(self, sems):
        self.sems, self.used = sems, 0

    def make(self, src, dst):
        self.used += 1
        return pltpu.make_async_copy(src, dst, self.sems.at[self.used - 1])

    def start(self, src, dst):
        copy = self.make(src, dst)
        copy.start()
        return copy


def wait_all(copies):
    for c in copies:
        c.wait()


def assemble(place, parts, first, copy_one, scatter=False):
    line, ahead, behind, low, high = parts
    x, z = place[0], place[1]
    copies = []
    for i, step in enumerate(STEPS):
        for j, inner in enumerate(STEPS):
            if step == 0:
                ref = line.at[j]
            elif step == 1:
                ref = ahead.at[j]
            elif step == -1:
                ref = behind.at[j]
            else:
                ref = low.at[j] if j < 2 else high.at[j - 2]
            if scatter:
                ref = pieces_at(*parts, step, j)
            if first == "z":
                dx, dz = step, inner
            else:
                dx, dz = inner, step
            copies += copy_one(ref, (x + dx + 4) % 4, (z + dz + 4) % 4)
    return copies


def at_rows(index, size):
    return pl.ds(pl.multiple_of(index * size, size), size)


def take_weights(copies, place, parts, wqkv):
    from_a = assemble(
        place, parts[:5], "z",
        lambda ref, x, z: [copies.start(ref, wqkv.at[at_rows(x * 4 + z, 80), pl.ds(0, 1280)])],
    )
    from_b = assemble(
        place, parts[5:], "x",
        lambda ref, x, z: [
            copies.start(ref.at[:, pl.ds(0, 640)], wqkv.at[at_rows(x * 4 + z, 80), pl.ds(1280, 640)])
        ],
    )
    return from_a, from_b


def take_out(copies, place, parts, wout):
    return assemble(
        place, parts, "x",
        lambda ref, x, z: [copies.start(ref.at[:, pl.ds(640, 640)], wout.at[at_rows(x * 4 + z, 80)])],
    )


def forward_kernel(place, own, sib, a0, a1, a2, a3, a4, b0, b1, b2, b3, b4,
                   probs_out, qkv_out, attended, wqkv, both, scores, probs, qkv, sems):
    copies = Copies(sems)
    from_a, from_b = take_weights(copies, place, (a0, a1, a2, a3, a4, b0, b1, b2, b3, b4), wqkv)
    both[:ROWS, :] = own[:, :D]
    both[ROWS:, :] = sib[:, :D]
    wait_all(from_a)

    def project(col):
        qkv[:, col] = dot(both[...], wqkv[:, col]).astype(BF)

    @pl.loop(0, 5)
    def _(t):
        project(at_rows(t, 256))

    wait_all(from_b)
    project(pl.ds(1280, 256))
    project(pl.ds(1536, 256))
    project(pl.ds(1792, 128))
    out_copies = [copies.start(qkv, qkv_out)]
    scale = HD ** (-0.5)

    @pl.loop(0, 4)
    def _(w):
        rows = at_rows(w, WIN)
        local = at_rows(w % 2, WIN)
        kinds = jnp.where(w < 2, own[local, D:].astype(F32), sib[local, D:].astype(F32)).astype(BF)
        allowed = dot_nt(kinds, kinds) > 0.5
        outs = []
        for group in range(0, HPC, 8):
            heads = [(h, h * HD, (h + 1) * HD) for h in range(group, group + 8)]
            for h, a, b in heads:
                scores[h] = dot_nt(qkv[rows, HALF + a:HALF + b], qkv[rows, a:b])
            for h, a, b in heads:
                s = jnp.where(allowed, scores[h] * scale, -1e30)
                e = jnp.exp(s - jnp.max(s, axis=0, keepdims=True))
                probs[w, h] = e * (1.0 / jnp.sum(e, axis=0, keepdims=True))
            for h, a, b in heads:
                outs.append(dot_tn(probs[w, h].astype(BF), qkv[rows, 2 * HALF + a:2 * HALF + b]).astype(BF))
        attended[rows, :] = jnp.concatenate(outs, axis=1)

    out_copies.append(copies.start(probs, probs_out))
    wait_all(out_copies)


def embed_kernel(place, attended, other, ordered, extra, sib_extra, b0, b1, b2, b3, b4, out, wout, sems):
    wait_all(take_out(Copies(sems), place, (b0, b1, b2, b3, b4), wout))
    here, there = at_rows(place[2], HALF), at_rows(1 - place[2], HALF)
    mine = dot(attended[:ROWS, :], wout[here, :]) + dot(other[ROWS:, :], wout[there, :])
    theirs = dot(attended[ROWS:, :], wout[here, :]) + dot(other[:ROWS, :], wout[there, :])
    mine = (half_of(place, ordered[...].astype(F32)) + mine).astype(BF)
    theirs = (sib_extra[:, SLOTS:].astype(F32) + theirs).astype(BF)
    total = dot_tn(extra[:, :SLOTS], mine) + dot_tn(sib_extra[:, :SLOTS], theirs)
    out[...] = total.astype(BF)


def pick_kernel(place, returned, extra, sib_extra, b0, b1, b2, b3, b4, grads, mine, theirs, wout, sems):
    copies = take_out(Copies(sems), place, (b0, b1, b2, b3, b4), wout)
    grads[:ROWS, :] = dot(extra[:, :SLOTS], returned[...]).astype(BF)
    grads[ROWS:, :] = dot(sib_extra[:, :SLOTS], returned[...]).astype(BF)
    wait_all(copies)
    mine[...] = dot_nt(grads[...], wout[at_rows(place[2], HALF), :])
    theirs[...] = dot_nt(grads[...], wout[at_rows(1 - place[2], HALF), :]).astype(BF)


def turn_kernel(own, sib, out):
    out[:, :ROWS] = own[:, :D].T
    out[:, ROWS:] = sib[:, :D].T


def pieces_at(own, up, down, next_up, next_down, step, inner):
    if step == 0:
        return own.at[inner]
    if step == 1:
        return next_up.at[inner] if inner < 2 else up.at[inner]
    if step == -1:
        return down.at[inner + 2] if inner < 2 else next_down.at[inner - 2]
    return up.at[inner] if inner < 2 else down.at[inner - 2]


def backward_kernel(place, grads_hbm, ga_mine, ga_other, normed_hbm, probs_hbm, qkv_hbm, attended_hbm, other_hbm,
                    gqkv_out, aown, aup, adown, alow, ahigh, bown, bup, bdown, blow, bhigh,
                    grads, gatt, ga, gb, terms, oterms, scores, small, normed_t, attended, other, attended_t,
                    probs, qkv, gqkv, sems):
    copies = Copies(sems)
    grads_in = [
        copies.start(ga_mine, ga),
        copies.start(ga_other.at[pl.ds(ROWS, ROWS)], gb.at[pl.ds(0, ROWS)]),
        copies.start(ga_other.at[pl.ds(0, ROWS)], gb.at[pl.ds(ROWS, ROWS)]),
    ]
    second_in = [
        copies.start(attended_hbm, attended),
        copies.start(other_hbm.at[pl.ds(ROWS, ROWS)], other.at[pl.ds(0, ROWS)]),
        copies.start(other_hbm.at[pl.ds(0, ROWS)], other.at[pl.ds(ROWS, ROWS)]),
        copies.start(grads_hbm, grads),
    ]
    first_in = [copies.start(qkv_hbm, qkv), copies.start(probs_hbm, probs)]
    last_in = copies.start(normed_hbm, normed_t)
    wait_all(grads_in)
    gatt[...] = (ga[...] + gb[...].astype(F32)).astype(BF)
    wait_all(second_in)
    attended_t[at_rows(place[2], HALF), :] = attended[...].T
    attended_t[at_rows(1 - place[2], HALF), :] = other[...].T
    for r in range(5):
        rows = slice(r * 256, (r + 1) * 256)
        oterms[rows, :] = dot(attended_t[rows, :], grads[...]).astype(BF)

    out_copies = assemble(
        place, (bown, bup, bdown, blow, bhigh), "x",
        lambda ref, x, z: [copies.start(oterms.at[at_rows(x * 4 + z, 80)], ref.at[:, pl.ds(640, 640)])],
        scatter=True,
    )
    scale = HD ** (-0.5)
    wait_all(first_in)

    @pl.loop(0, 4)
    def _(w):
        rows = at_rows(w, WIN)
        to_query, to_key, to_value = [], [], []
        for group in range(0, HPC, 8):
            heads = [(h, h * HD, (h + 1) * HD) for h in range(group, group + 8)]
            for h, a, b in heads:
                scores[h] = dot_nt(qkv[rows, 2 * HALF + a:2 * HALF + b], gatt[rows, a:b])
            for h, a, b in heads:
                to_value.append(dot(probs[w, h].astype(BF), gatt[rows, a:b]).astype(BF))
            for h, a, b in heads:
                p = probs[w, h]
                g = scores[h]
                inner = jnp.sum(p * g, axis=0, keepdims=True)
                small[h] = (p * (g - inner) * scale).astype(BF)
            for h, a, b in heads:
                to_key.append(dot(small[h], qkv[rows, a:b]).astype(BF))
                to_query.append(dot_tn(small[h], qkv[rows, HALF + a:HALF + b]).astype(BF))
        gqkv[rows, :HALF] = jnp.concatenate(to_query, axis=1)
        gqkv[rows, HALF:2 * HALF] = jnp.concatenate(to_key, axis=1)
        gqkv[rows, 2 * HALF:] = jnp.concatenate(to_value, axis=1)

    out_copies.append(copies.start(gqkv, gqkv_out))
    last_in.wait()

    def weigh(col):
        terms[:, col] = dot(normed_t[...], gqkv[:, col]).astype(BF)

    @pl.loop(0, 5)
    def _(t):
        weigh(at_rows(t, 256))

    out_copies += assemble(
        place, (aown, aup, adown, alow, ahigh), "z",
        lambda ref, x, z: [copies.start(terms.at[at_rows(x * 4 + z, 80), pl.ds(0, 1280)], ref)],
        scatter=True,
    )
    weigh(pl.ds(1280, 256))
    weigh(pl.ds(1536, 256))
    weigh(pl.ds(1792, 128))
    out_copies += assemble(
        place, (bown, bup, bdown, blow, bhigh), "x",
        lambda ref, x, z: [
            copies.start(terms.at[at_rows(x * 4 + z, 80), pl.ds(1280, 640)], ref.at[:, pl.ds(0, 640)])
        ],
        scatter=True,
    )
    wait_all(out_copies)


def norm_grad_kernel(place, gqkv, a0, a1, a2, a3, a4, b0, b1, b2, b3, b4, mine, theirs, wqkv, sems):
    from_a, from_b = take_weights(Copies(sems), place, (a0, a1, a2, a3, a4, b0, b1, b2, b3, b4), wqkv)
    wait_all(from_a + from_b)
    for t in range(5):
        col = slice(t * 256, (t + 1) * 256)
        part = dot_nt(gqkv[...], wqkv[col, :])
        mine[:, col] = part[:ROWS]
        theirs[:, col] = part[ROWS:].astype(BF)


def finish_kernel(place, mine, theirs, ordered, gain, grads, other, order_t, out):
    rows = lax.broadcasted_iota(jnp.int32, (ROWS, ROWS), 0)
    back = (order_t[...] == rows).astype(BF)
    rowsw = ordered[...].astype(F32)
    spread = lax.rsqrt(jnp.mean(rowsw * rowsw, axis=1, keepdims=True) + EPSILON)
    scaled = rowsw * spread
    normed = (mine[...] + theirs[...].astype(F32)).astype(BF).astype(F32)
    u = normed * gain[...]
    layer = (u - scaled * jnp.mean(u * scaled, axis=1, keepdims=True)) * spread
    here, there = grads[:ROWS, :].astype(F32), other[...].astype(F32)
    first = place[2] == 0
    window = (jnp.where(first, here, there) + layer[:, :HALF]).astype(BF)
    out[:, :HALF] = dot(back, window).astype(BF)
    window = (jnp.where(first, there, here) + layer[:, HALF:]).astype(BF)
    out[:, HALF:] = dot(back, window).astype(BF)


def body(patches, ln_gain, qkv_weight, out_weight, image_counts, window_order, owner_map, owner_grads):
    index = lax.axis_index("enc")
    x, z, core = index // 8, (index // 2) % 4, index % 2
    place = jnp.stack([x, z, core])
    gain = ln_gain.reshape(1, D)
    order = window_order.reshape(ROWS, 1)
    order_t = window_order.reshape(1, ROWS)

    first_core = core == 0
    with jax.named_scope("weights"):

        def columns(half):
            start = half * HALF
            parts = [qkv_weight[:, t * D + start :][:, :HALF] for t in range(3)]
            return jnp.concatenate(parts + [out_weight[:, start : start + HALF]], axis=1)

        low, high = columns(0), columns(1)
        got = to_sibling(jnp.where(first_core, high, low))
        keep = jnp.where(first_core, low, high)
        shard = jnp.where(first_core, jnp.concatenate([keep, got]), jnp.concatenate([got, keep]))
        line_a = gather_line(shard[:, : 2 * HALF], "z")
        line_b = gather_line(shard[:, 2 * HALF :], "x")
        part_a = gather_rest(line_a, "x")
        part_b = gather_rest(line_b, "z")
    with jax.named_scope("prepare"):
        naug, extra, ordered = call(
            prepare_kernel,
            [((ROWS, D + 128), BF), ((ROWS, SLOTS + HALF), BF), ((ROWS, D), BF)],
            (place, image_counts, patches, gain, order, owner_map),
            "ssvvvv",
        )
        nsib, sib_extra = to_sibling(naug), to_sibling(extra)
        (normed_t,) = call(turn_kernel, [((D, 512), BF)], (naug, nsib), "vv")
    with jax.named_scope("grads_in"):
        sent = owner_grads.reshape(64, 8, 2, HALF).transpose(0, 2, 1, 3).reshape(SLOTS, HALF)
        sent, part_a, part_b, normed_t, sib_extra = lax.optimization_barrier((sent, part_a, part_b, normed_t, sib_extra))
        returned = lax.all_to_all(sent, ("grp", "enc"), split_axis=0, concat_axis=0, tiled=True)
    with jax.named_scope("forward"):
        probs, qkv, attended = call(
            forward_kernel,
            [((4, HPC, WIN, WIN), F32), ((512, 3 * HALF), BF), ((512, HALF), BF)],
            (place, naug, nsib, *part_a, *part_b),
            "svv" + "a" * 10,
            "aav",
            scratch=[
                pltpu.VMEM((D, 3 * HALF), BF),
                pltpu.VMEM((512, D), BF),
                pltpu.VMEM((HPC, WIN, WIN), F32),
                pltpu.VMEM((4, HPC, WIN, WIN), F32),
                pltpu.VMEM((512, 3 * HALF), BF),
                pltpu.SemaphoreType.DMA((34,)),
            ],
            us=12,
        )
        other = to_sibling(attended)
        (outgoing,) = call(
            embed_kernel,
            [((SLOTS, HALF), BF)],
            (place, attended, other, ordered, extra, sib_extra, *part_b),
            "svvvvv" + "a" * 5,
            scratch=[pltpu.VMEM((D, HALF), BF), pltpu.SemaphoreType.DMA((16,))],
        )
    with jax.named_scope("grads_in"):
        returned, outgoing = lax.optimization_barrier((returned, outgoing))
        grads, ga_mine, ga_theirs = call(
            pick_kernel,
            [((512, HALF), BF), ((512, HALF), F32), ((512, HALF), BF)],
            (place, returned, extra, sib_extra, *part_b),
            "svvv" + "a" * 5,
            scratch=[pltpu.VMEM((D, HALF), BF), pltpu.SemaphoreType.DMA((16,))],
        )
        ga_mine, ga_theirs, outgoing = lax.optimization_barrier((ga_mine, ga_theirs, outgoing))
        ga_other = to_sibling(ga_theirs)
    with jax.named_scope("backward"):
        pieces = [((4, 80, D), BF)] * 3 + [((2, 80, D), BF)] * 2
        gqkv, *terms = call(
            backward_kernel,
            [((512, 3 * HALF), BF)] + pieces + pieces,
            (place, grads, ga_mine, ga_other, normed_t, probs, qkv, attended, other),
            "s" + "a" * 8,
            "a" * 11,
            scratch=[
                pltpu.VMEM((512, HALF), BF),
                pltpu.VMEM((512, HALF), BF),
                pltpu.VMEM((512, HALF), F32),
                pltpu.VMEM((512, HALF), BF),
                pltpu.VMEM((D, 3 * HALF), BF),
                pltpu.VMEM((D, HALF), BF),
                pltpu.VMEM((HPC, WIN, WIN), F32),
                pltpu.VMEM((HPC, WIN, WIN), BF),
                pltpu.VMEM((D, 512), BF),
                pltpu.VMEM((512, HALF), BF),
                pltpu.VMEM((512, HALF), BF),
                pltpu.VMEM((D, 512), BF),
                pltpu.VMEM((4, HPC, WIN, WIN), F32),
                pltpu.VMEM((512, 3 * HALF), BF),
                pltpu.VMEM((512, 3 * HALF), BF),
                pltpu.SemaphoreType.DMA((60,)),
            ],
            us=1,
        )
    with jax.named_scope("rows_out"):
        owner_rows = lax.all_to_all(outgoing, ("grp", "enc"), split_axis=0, concat_axis=0, tiled=True)
    with jax.named_scope("weight_grads"):
        up_a, down_a = scatter_first(*terms[1:3], "x")
        up_b, down_b = scatter_first(*terms[6:8], "z")
    with jax.named_scope("norm_grad"):
        tick = hop(terms[1][0, :16, :128], "y", 1)
        gqkv, tick = lax.optimization_barrier((gqkv, tick))
        nmine, ntheirs = call(
            norm_grad_kernel,
            [((ROWS, D), F32), ((ROWS, D), BF)],
            (place, gqkv, *part_a, *part_b),
            "sv" + "a" * 10,
            scratch=[pltpu.VMEM((D, 3 * HALF), BF), pltpu.SemaphoreType.DMA((32,))],
            us=1,
        )
    with jax.named_scope("weight_grads"):
        up_a, down_a, ntheirs, owner_rows = lax.optimization_barrier((up_a, down_a, ntheirs, owner_rows))
        sum_a = scatter_second(terms[0], up_a, down_a, *terms[3:5], "x", "z")
        sum_b = scatter_second(terms[5], up_b, down_b, *terms[8:], "z", "x")
    with jax.named_scope("norm_grad"):
        nfrom = to_sibling(ntheirs)
        grads_other = to_sibling(grads[ROWS:])
        (patch_grads,) = call(
            finish_kernel,
            [((ROWS, D), BF)],
            (place, nmine, nfrom, ordered, gain, grads, grads_other, order_t),
            "svvvvvvv",
        )
    with jax.named_scope("back_to_rows"):
        mine = jnp.concatenate([sum_a, sum_b], axis=1).astype(BF)
        low, high = mine[:40], mine[40:]
        got = to_sibling(jnp.where(first_core, high, low))
        keep = jnp.where(first_core, low, high)
        low, high = jnp.where(first_core, keep, got), jnp.where(first_core, got, keep)
        blocks = jnp.stack(
            [jnp.concatenate([low[:, t * HALF : (t + 1) * HALF], high[:, t * HALF : (t + 1) * HALF]], axis=1) for t in range(4)]
        )
    with jax.named_scope("rows_out"):
        owner_rows = owner_rows.reshape(64, 2, 8, HALF).transpose(0, 2, 1, 3).reshape(512, D)
        blocks, owner_rows = lax.optimization_barrier((blocks, owner_rows))
    with jax.named_scope("over_groups"):
        me = lax.axis_index("grp")

        def block(step):
            return lax.dynamic_index_in_dim(blocks, (me + step + 4) % 4, 0, keepdims=False)

        total = block(0).astype(F32)
        for step in STEPS[1:]:
            total = total + hop(block(step), "y", step).astype(F32)
        total = total.astype(BF)
        every = [total] + [hop(total, "y", -step) for step in STEPS[1:]]
        factor = 1.0 / math.sqrt(ROWS * 128)

        def summed(t):
            step = (t - me + 4) % 4
            value = jnp.where(
                step == 0, every[0], jnp.where(step == 1, every[1], jnp.where(step == 3, every[2], every[3]))
            )
            return value.astype(F32) * factor

        qkv_grad = jnp.concatenate([summed(t) for t in range(3)], axis=1)
        out_grad = summed(3)
    return owner_rows, patch_grads, qkv_grad, out_grad


def solution(mesh):
    rows = P(("grp", "enc"), None)
    in_specs = (rows, P(), P("enc", None), P("enc", None), rows, rows, rows, rows)
    out_specs = (rows, rows, P("enc", None), P("enc", None))
    return jax.shard_map(body, mesh=mesh, in_specs=in_specs, out_specs=out_specs, check_vma=False)
```

```python
import math

import jax
import jax.numpy as jnp
from jax import lax
from jax.experimental import pallas as pl
from jax.experimental.pallas import tpu as pltpu
from jax.sharding import PartitionSpec as P

HEADS = 16
HD = 80
WIN = 128
EPSILON = 1e-06
D = 1280
ROWS = 256
HALF = 640
HPC = HEADS // 2
SLOTS = 1024
BF = jnp.bfloat16
F32 = jnp.float32
VMEM_LIMIT = 58 * 1024 * 1024
STEPS = (0, 1, -1, 2)


def ring(axis, step):
    pairs = []
    for x in range(4):
        for z in range(4):
            for c in range(2):
                to = ((x + step) % 4, z) if axis == "x" else (x, (z + step) % 4)
                pairs.append(((x * 4 + z) * 2 + c, (to[0] * 4 + to[1]) * 2 + c))
    return pairs


def hop(value, axis, step):
    if axis == "y":
        return lax.ppermute(value, "grp", [(i, (i + step) % 4) for i in range(4)])
    return lax.ppermute(value, "enc", ring(axis, step))


def to_sibling(value):
    return lax.ppermute(value, "enc", [(i, i ^ 1) for i in range(32)])


def gather_line(shard, first):
    behind = hop(shard, first, 1)
    ahead = hop(shard, first, -1)
    across = hop(shard, first, 2)
    return jnp.stack([shard, ahead, behind, across])


def gather_rest(line, second):
    line_behind = hop(line, second, 1)
    line_ahead = hop(line, second, -1)
    far_low = hop(line_behind[:2], second, 1)
    far_high = hop(line_ahead[2:], second, -1)
    return line, line_ahead, line_behind, far_low, far_high


def add(*values):
    total = values[0].astype(F32)
    for v in values[1:]:
        total = total + v.astype(F32)
    return total


def scatter_first(up, down, axis):
    return hop(up, axis, 1), hop(down, axis, -1)


def scatter_second(own, from_up, from_down, next_up, next_down, first, second):
    last_up = hop(add(next_up, from_up[:2]).astype(BF), first, 1)
    last_down = hop(add(next_down, from_down[:2]).astype(BF), first, -1)
    total = jnp.concatenate([add(own[:2], last_up, from_down[2:]), add(own[2:], from_up[2:], last_down)])
    rounded = total.astype(BF)
    one = hop(rounded[1], second, 1)
    two = hop(rounded[2], second, -1)
    three = hop(rounded[3], second, 2)
    return add(total[0], one, two, three)


def dot(a, b):
    return jnp.dot(a, b, preferred_element_type=F32)


def dot_nt(a, b):
    return lax.dot_general(a, b, (((1,), (1,)), ((), ())), preferred_element_type=F32)


def dot_tn(a, b):
    return lax.dot_general(a, b, (((0,), (0,)), ((), ())), preferred_element_type=F32)


def call(kernel, outs, ins, in_spaces, out_spaces=None, scratch=(), us=3):
    spaces = {"v": pltpu.VMEM, "s": pltpu.SMEM, "a": pltpu.HBM}
    out_spaces = out_spaces or "v" * len(outs)
    return pl.pallas_call(
        kernel,
        out_shape=[jax.ShapeDtypeStruct(s, t) for s, t in outs],
        in_specs=[pl.BlockSpec(memory_space=spaces[c]) for c in in_spaces],
        out_specs=[pl.BlockSpec(memory_space=spaces[c]) for c in out_spaces],
        scratch_shapes=list(scratch),
        compiler_params=pltpu.CompilerParams(vmem_limit_bytes=VMEM_LIMIT),
        cost_estimate=pl.CostEstimate(flops=us * 10**9, bytes_accessed=us * 3 * 10**6, transcendentals=0),
    )(*ins)


def half_of(place, value):
    return jnp.where(place[2] == 0, value[:, :HALF], value[:, HALF:])


def prepare_kernel(place, counts, patches, gain, order, owners, naug, extra, ordered):
    rows = lax.broadcasted_iota(jnp.int32, (ROWS, ROWS), 1)
    perm = (order[...] == rows).astype(BF)
    row = lax.broadcasted_iota(jnp.int32, (ROWS, 128), 0)
    lane = lax.broadcasted_iota(jnp.int32, (ROWS, 128), 1)
    image = jnp.zeros((ROWS, 128), jnp.int32)
    end = 0
    for k in range(4):
        end = end + counts[0, k]
        image = image + (row >= end).astype(jnp.int32)
    kinds = dot(perm, (image == lane).astype(BF)).astype(BF)
    named = (owners[...] == lane).astype(BF)
    earlier = (rows < lax.broadcasted_iota(jnp.int32, (ROWS, ROWS), 0)).astype(BF)
    before = dot(earlier, named)
    slot = jnp.sum(before * named.astype(F32), axis=1, keepdims=True).astype(jnp.int32)
    target = owners[...] * 8 + place[2] * 4 + slot
    slots = lax.broadcasted_iota(jnp.int32, (ROWS, SLOTS), 1)
    extra[:, :SLOTS] = dot(perm, (target == slots).astype(BF)).astype(BF)
    rowsw = dot(perm, patches[...])
    ordered[...] = rowsw.astype(BF)
    extra[:, SLOTS:] = jnp.where(place[2] == 0, rowsw[:, HALF:], rowsw[:, :HALF]).astype(BF)
    spread = lax.rsqrt(jnp.mean(rowsw * rowsw, axis=1, keepdims=True) + EPSILON)
    naug[:, :D] = (rowsw * spread * gain[...]).astype(BF)
    naug[:, D:] = kinds


class Copies:
    def __init__(self, sems):
        self.sems, self.used = sems, 0

    def make(self, src, dst):
        self.used += 1
        return pltpu.make_async_copy(src, dst, self.sems.at[self.used - 1])

    def start(self, src, dst):
        copy = self.make(src, dst)
        copy.start()
        return copy


def wait_all(copies):
    for c in copies:
        c.wait()


def assemble(place, parts, first, copy_one, scatter=False):
    line, ahead, behind, low, high = parts
    x, z = place[0], place[1]
    copies = []
    for i, step in enumerate(STEPS):
        for j, inner in enumerate(STEPS):
            if step == 0:
                ref = line.at[j]
            elif step == 1:
                ref = ahead.at[j]
            elif step == -1:
                ref = behind.at[j]
            else:
                ref = low.at[j] if j < 2 else high.at[j - 2]
            if scatter:
                ref = pieces_at(*parts, step, j)
            if first == "z":
                dx, dz = step, inner
            else:
                dx, dz = inner, step
            copies += copy_one(ref, (x + dx + 4) % 4, (z + dz + 4) % 4)
    return copies


def at_rows(index, size):
    return pl.ds(pl.multiple_of(index * size, size), size)


def take_weights(copies, place, parts, wqkv):
    from_a = assemble(
        place, parts[:5], "z",
        lambda ref, x, z: [copies.start(ref, wqkv.at[at_rows(x * 4 + z, 80), pl.ds(0, 1280)])],
    )
    from_b = assemble(
        place, parts[5:], "x",
        lambda ref, x, z: [
            copies.start(ref.at[:, pl.ds(0, 640)], wqkv.at[at_rows(x * 4 + z, 80), pl.ds(1280, 640)])
        ],
    )
    return from_a, from_b


def take_out(copies, place, parts, wout):
    return assemble(
        place, parts, "x",
        lambda ref, x, z: [copies.start(ref.at[:, pl.ds(640, 640)], wout.at[at_rows(x * 4 + z, 80)])],
    )


def forward_kernel(place, own, sib, a0, a1, a2, a3, a4, b0, b1, b2, b3, b4,
                   probs_out, qkv_out, attended, wqkv, both, scores, probs, qkv, sems):
    copies = Copies(sems)
    from_a, from_b = take_weights(copies, place, (a0, a1, a2, a3, a4, b0, b1, b2, b3, b4), wqkv)
    both[:ROWS, :] = own[:, :D]
    both[ROWS:, :] = sib[:, :D]
    wait_all(from_a)

    def project(col):
        qkv[:, col] = dot(both[...], wqkv[:, col]).astype(BF)

    @pl.loop(0, 5)
    def _(t):
        project(at_rows(t, 256))

    wait_all(from_b)
    project(pl.ds(1280, 256))
    project(pl.ds(1536, 256))
    project(pl.ds(1792, 128))
    out_copies = [copies.start(qkv, qkv_out)]
    scale = HD ** (-0.5)

    @pl.loop(0, 4)
    def _(w):
        rows = at_rows(w, WIN)
        local = at_rows(w % 2, WIN)
        kinds = jnp.where(w < 2, own[local, D:].astype(F32), sib[local, D:].astype(F32)).astype(BF)
        allowed = dot_nt(kinds, kinds) > 0.5
        outs = []
        for group in range(0, HPC, 8):
            heads = [(h, h * HD, (h + 1) * HD) for h in range(group, group + 8)]
            for h, a, b in heads:
                scores[h] = dot_nt(qkv[rows, HALF + a:HALF + b], qkv[rows, a:b])
            for h, a, b in heads:
                s = jnp.where(allowed, scores[h] * scale, -1e30)
                e = jnp.exp(s - jnp.max(s, axis=0, keepdims=True))
                probs[w, h] = e * (1.0 / jnp.sum(e, axis=0, keepdims=True))
            for h, a, b in heads:
                outs.append(dot_tn(probs[w, h].astype(BF), qkv[rows, 2 * HALF + a:2 * HALF + b]).astype(BF))
        attended[rows, :] = jnp.concatenate(outs, axis=1)

    out_copies.append(copies.start(probs, probs_out))
    wait_all(out_copies)


def embed_kernel(place, attended, other, ordered, extra, sib_extra, b0, b1, b2, b3, b4, out, wout, sems):
    wait_all(take_out(Copies(sems), place, (b0, b1, b2, b3, b4), wout))
    here, there = at_rows(place[2], HALF), at_rows(1 - place[2], HALF)
    mine = dot(attended[:ROWS, :], wout[here, :]) + dot(other[ROWS:, :], wout[there, :])
    theirs = dot(attended[ROWS:, :], wout[here, :]) + dot(other[:ROWS, :], wout[there, :])
    mine = (half_of(place, ordered[...].astype(F32)) + mine).astype(BF)
    theirs = (sib_extra[:, SLOTS:].astype(F32) + theirs).astype(BF)
    total = dot_tn(extra[:, :SLOTS], mine) + dot_tn(sib_extra[:, :SLOTS], theirs)
    out[...] = total.astype(BF)


def pick_kernel(place, returned, extra, sib_extra, b0, b1, b2, b3, b4, grads, mine, theirs, wout, sems):
    copies = take_out(Copies(sems), place, (b0, b1, b2, b3, b4), wout)
    grads[:ROWS, :] = dot(extra[:, :SLOTS], returned[...]).astype(BF)
    grads[ROWS:, :] = dot(sib_extra[:, :SLOTS], returned[...]).astype(BF)
    wait_all(copies)
    mine[...] = dot_nt(grads[...], wout[at_rows(place[2], HALF), :]).astype(BF)
    theirs[...] = dot_nt(grads[...], wout[at_rows(1 - place[2], HALF), :]).astype(BF)


def turn_kernel(own, sib, out):
    out[:, :ROWS] = own[:, :D].T
    out[:, ROWS:] = sib[:, :D].T


def pieces_at(own, up, down, next_up, next_down, step, inner):
    if step == 0:
        return own.at[inner]
    if step == 1:
        return next_up.at[inner] if inner < 2 else up.at[inner]
    if step == -1:
        return down.at[inner + 2] if inner < 2 else next_down.at[inner - 2]
    return up.at[inner] if inner < 2 else down.at[inner - 2]


def backward_kernel(place, grads_hbm, ga_mine, ga_other, normed_hbm, probs_hbm, qkv_hbm, attended_hbm, other_hbm,
                    gqkv_out, aown, aup, adown, alow, ahigh, bown, bup, bdown, blow, bhigh,
                    grads, gatt, ga, gb, terms, oterms, scores, small, normed_t, attended, other, attended_t,
                    probs, qkv, gqkv, sems):
    copies = Copies(sems)
    grads_in = [
        copies.start(ga_mine, ga),
        copies.start(ga_other.at[pl.ds(ROWS, ROWS)], gb.at[pl.ds(0, ROWS)]),
        copies.start(ga_other.at[pl.ds(0, ROWS)], gb.at[pl.ds(ROWS, ROWS)]),
    ]
    second_in = [
        copies.start(attended_hbm, attended),
        copies.start(other_hbm.at[pl.ds(ROWS, ROWS)], other.at[pl.ds(0, ROWS)]),
        copies.start(other_hbm.at[pl.ds(0, ROWS)], other.at[pl.ds(ROWS, ROWS)]),
        copies.start(grads_hbm, grads),
    ]
    first_in = [copies.start(qkv_hbm, qkv), copies.start(probs_hbm, probs)]
    last_in = copies.start(normed_hbm, normed_t)
    wait_all(grads_in)
    gatt[...] = add(ga[...], gb[...]).astype(BF)
    wait_all(second_in)
    attended_t[at_rows(place[2], HALF), :] = attended[...].T
    attended_t[at_rows(1 - place[2], HALF), :] = other[...].T
    for r in range(5):
        rows = slice(r * 256, (r + 1) * 256)
        oterms[rows, :] = dot(attended_t[rows, :], grads[...]).astype(BF)

    out_copies = assemble(
        place, (bown, bup, bdown, blow, bhigh), "x",
        lambda ref, x, z: [copies.start(oterms.at[at_rows(x * 4 + z, 80)], ref.at[:, pl.ds(640, 640)])],
        scatter=True,
    )
    scale = HD ** (-0.5)
    wait_all(first_in)

    @pl.loop(0, 4)
    def _(w):
        rows = at_rows(w, WIN)
        to_query, to_key, to_value = [], [], []
        for group in range(0, HPC, 8):
            heads = [(h, h * HD, (h + 1) * HD) for h in range(group, group + 8)]
            for h, a, b in heads:
                scores[h] = dot_nt(qkv[rows, 2 * HALF + a:2 * HALF + b], gatt[rows, a:b])
            for h, a, b in heads:
                to_value.append(dot(probs[w, h].astype(BF), gatt[rows, a:b]).astype(BF))
            for h, a, b in heads:
                p = probs[w, h]
                g = scores[h]
                inner = jnp.sum(p * g, axis=0, keepdims=True)
                small[h] = (p * (g - inner) * scale).astype(BF)
            for h, a, b in heads:
                to_key.append(dot(small[h], qkv[rows, a:b]).astype(BF))
                to_query.append(dot_tn(small[h], qkv[rows, HALF + a:HALF + b]).astype(BF))
        gqkv[rows, :HALF] = jnp.concatenate(to_query, axis=1)
        gqkv[rows, HALF:2 * HALF] = jnp.concatenate(to_key, axis=1)
        gqkv[rows, 2 * HALF:] = jnp.concatenate(to_value, axis=1)

    out_copies.append(copies.start(gqkv, gqkv_out))
    last_in.wait()

    def weigh(col):
        terms[:, col] = dot(normed_t[...], gqkv[:, col]).astype(BF)

    @pl.loop(0, 5)
    def _(t):
        weigh(at_rows(t, 256))

    out_copies += assemble(
        place, (aown, aup, adown, alow, ahigh), "z",
        lambda ref, x, z: [copies.start(terms.at[at_rows(x * 4 + z, 80), pl.ds(0, 1280)], ref)],
        scatter=True,
    )
    weigh(pl.ds(1280, 256))
    weigh(pl.ds(1536, 256))
    weigh(pl.ds(1792, 128))
    out_copies += assemble(
        place, (bown, bup, bdown, blow, bhigh), "x",
        lambda ref, x, z: [
            copies.start(terms.at[at_rows(x * 4 + z, 80), pl.ds(1280, 640)], ref.at[:, pl.ds(0, 640)])
        ],
        scatter=True,
    )
    wait_all(out_copies)


def norm_grad_kernel(place, gqkv, a0, a1, a2, a3, a4, b0, b1, b2, b3, b4, mine, theirs, wqkv, sems):
    from_a, from_b = take_weights(Copies(sems), place, (a0, a1, a2, a3, a4, b0, b1, b2, b3, b4), wqkv)
    wait_all(from_a + from_b)
    for t in range(5):
        col = slice(t * 256, (t + 1) * 256)
        part = dot_nt(gqkv[...], wqkv[col, :])
        mine[:, col] = part[:ROWS]
        theirs[:, col] = part[ROWS:].astype(BF)


def finish_kernel(place, mine, theirs, ordered, gain, grads, other, order_t, out):
    rows = lax.broadcasted_iota(jnp.int32, (ROWS, ROWS), 0)
    back = (order_t[...] == rows).astype(BF)
    rowsw = ordered[...].astype(F32)
    spread = lax.rsqrt(jnp.mean(rowsw * rowsw, axis=1, keepdims=True) + EPSILON)
    scaled = rowsw * spread
    normed = (mine[...] + theirs[...].astype(F32)).astype(BF).astype(F32)
    u = normed * gain[...]
    layer = (u - scaled * jnp.mean(u * scaled, axis=1, keepdims=True)) * spread
    here, there = grads[:ROWS, :].astype(F32), other[...].astype(F32)
    first = place[2] == 0
    window = (jnp.where(first, here, there) + layer[:, :HALF]).astype(BF)
    out[:, :HALF] = dot(back, window).astype(BF)
    window = (jnp.where(first, there, here) + layer[:, HALF:]).astype(BF)
    out[:, HALF:] = dot(back, window).astype(BF)


def body(patches, ln_gain, qkv_weight, out_weight, image_counts, window_order, owner_map, owner_grads):
    index = lax.axis_index("enc")
    x, z, core = index // 8, (index // 2) % 4, index % 2
    place = jnp.stack([x, z, core])
    gain = ln_gain.reshape(1, D)
    order = window_order.reshape(ROWS, 1)
    order_t = window_order.reshape(1, ROWS)

    first_core = core == 0
    with jax.named_scope("weights"):

        def columns(half):
            start = half * HALF
            parts = [qkv_weight[:, t * D + start :][:, :HALF] for t in range(3)]
            return jnp.concatenate(parts + [out_weight[:, start : start + HALF]], axis=1)

        low, high = columns(0), columns(1)
        got = to_sibling(jnp.where(first_core, high, low))
        keep = jnp.where(first_core, low, high)
        shard = jnp.where(first_core, jnp.concatenate([keep, got]), jnp.concatenate([got, keep]))
        line_a = gather_line(shard[:, : 2 * HALF], "z")
        line_b = gather_line(shard[:, 2 * HALF :], "x")
        part_a = gather_rest(line_a, "x")
        part_b = gather_rest(line_b, "z")
    with jax.named_scope("prepare"):
        naug, extra, ordered = call(
            prepare_kernel,
            [((ROWS, D + 128), BF), ((ROWS, SLOTS + HALF), BF), ((ROWS, D), BF)],
            (place, image_counts, patches, gain, order, owner_map),
            "ssvvvv",
        )
        nsib, sib_extra = to_sibling(naug), to_sibling(extra)
        (normed_t,) = call(turn_kernel, [((D, 512), BF)], (naug, nsib), "vv")
    with jax.named_scope("grads_in"):
        sent = owner_grads.reshape(64, 8, 2, HALF).transpose(0, 2, 1, 3).reshape(SLOTS, HALF)
        sent, part_a, part_b, normed_t, sib_extra = lax.optimization_barrier((sent, part_a, part_b, normed_t, sib_extra))
        returned = lax.all_to_all(sent, ("grp", "enc"), split_axis=0, concat_axis=0, tiled=True)
    with jax.named_scope("forward"):
        probs, qkv, attended = call(
            forward_kernel,
            [((4, HPC, WIN, WIN), F32), ((512, 3 * HALF), BF), ((512, HALF), BF)],
            (place, naug, nsib, *part_a, *part_b),
            "svv" + "a" * 10,
            "aav",
            scratch=[
                pltpu.VMEM((D, 3 * HALF), BF),
                pltpu.VMEM((512, D), BF),
                pltpu.VMEM((HPC, WIN, WIN), F32),
                pltpu.VMEM((4, HPC, WIN, WIN), F32),
                pltpu.VMEM((512, 3 * HALF), BF),
                pltpu.SemaphoreType.DMA((34,)),
            ],
            us=12,
        )
        other = to_sibling(attended)
        (outgoing,) = call(
            embed_kernel,
            [((SLOTS, HALF), BF)],
            (place, attended, other, ordered, extra, sib_extra, *part_b),
            "svvvvv" + "a" * 5,
            scratch=[pltpu.VMEM((D, HALF), BF), pltpu.SemaphoreType.DMA((16,))],
        )
    with jax.named_scope("grads_in"):
        returned, outgoing = lax.optimization_barrier((returned, outgoing))
        grads, ga_mine, ga_theirs = call(
            pick_kernel,
            [((512, HALF), BF)] * 3,
            (place, returned, extra, sib_extra, *part_b),
            "svvv" + "a" * 5,
            scratch=[pltpu.VMEM((D, HALF), BF), pltpu.SemaphoreType.DMA((16,))],
        )
        ga_mine, ga_theirs, outgoing = lax.optimization_barrier((ga_mine, ga_theirs, outgoing))
        ga_other = to_sibling(ga_theirs)
    with jax.named_scope("backward"):
        pieces = [((4, 80, D), BF)] * 3 + [((2, 80, D), BF)] * 2
        gqkv, *terms = call(
            backward_kernel,
            [((512, 3 * HALF), BF)] + pieces + pieces,
            (place, grads, ga_mine, ga_other, normed_t, probs, qkv, attended, other),
            "s" + "a" * 8,
            "a" * 11,
            scratch=[
                pltpu.VMEM((512, HALF), BF),
                pltpu.VMEM((512, HALF), BF),
                pltpu.VMEM((512, HALF), BF),
                pltpu.VMEM((512, HALF), BF),
                pltpu.VMEM((D, 3 * HALF), BF),
                pltpu.VMEM((D, HALF), BF),
                pltpu.VMEM((HPC, WIN, WIN), F32),
                pltpu.VMEM((HPC, WIN, WIN), BF),
                pltpu.VMEM((D, 512), BF),
                pltpu.VMEM((512, HALF), BF),
                pltpu.VMEM((512, HALF), BF),
                pltpu.VMEM((D, 512), BF),
                pltpu.VMEM((4, HPC, WIN, WIN), F32),
                pltpu.VMEM((512, 3 * HALF), BF),
                pltpu.VMEM((512, 3 * HALF), BF),
                pltpu.SemaphoreType.DMA((60,)),
            ],
            us=1,
        )
    with jax.named_scope("rows_out"):
        owner_rows = lax.all_to_all(outgoing, ("grp", "enc"), split_axis=0, concat_axis=0, tiled=True)
    with jax.named_scope("weight_grads"):
        up_a, down_a = scatter_first(*terms[1:3], "x")
        up_b, down_b = scatter_first(*terms[6:8], "z")
    with jax.named_scope("norm_grad"):
        tick = hop(terms[1][0, :16, :128], "y", 1)
        gqkv, tick = lax.optimization_barrier((gqkv, tick))
        nmine, ntheirs = call(
            norm_grad_kernel,
            [((ROWS, D), F32), ((ROWS, D), BF)],
            (place, gqkv, *part_a, *part_b),
            "sv" + "a" * 10,
            scratch=[pltpu.VMEM((D, 3 * HALF), BF), pltpu.SemaphoreType.DMA((32,))],
            us=1,
        )
    with jax.named_scope("weight_grads"):
        up_a, down_a, ntheirs, owner_rows = lax.optimization_barrier((up_a, down_a, ntheirs, owner_rows))
        sum_a = scatter_second(terms[0], up_a, down_a, *terms[3:5], "x", "z")
        sum_b = scatter_second(terms[5], up_b, down_b, *terms[8:], "z", "x")
    with jax.named_scope("norm_grad"):
        nfrom = to_sibling(ntheirs)
        grads_other = to_sibling(grads[ROWS:])
        (patch_grads,) = call(
            finish_kernel,
            [((ROWS, D), BF)],
            (place, nmine, nfrom, ordered, gain, grads, grads_other, order_t),
            "svvvvvvv",
        )
    with jax.named_scope("back_to_rows"):
        mine = jnp.concatenate([sum_a, sum_b], axis=1).astype(BF)
        low, high = mine[:40], mine[40:]
        got = to_sibling(jnp.where(first_core, high, low))
        keep = jnp.where(first_core, low, high)
        low, high = jnp.where(first_core, keep, got), jnp.where(first_core, got, keep)
        blocks = jnp.stack(
            [jnp.concatenate([low[:, t * HALF : (t + 1) * HALF], high[:, t * HALF : (t + 1) * HALF]], axis=1) for t in range(4)]
        )
    with jax.named_scope("rows_out"):
        owner_rows = owner_rows.reshape(64, 2, 8, HALF).transpose(0, 2, 1, 3).reshape(512, D)
        blocks, owner_rows = lax.optimization_barrier((blocks, owner_rows))
    with jax.named_scope("over_groups"):
        me = lax.axis_index("grp")

        def block(step):
            return lax.dynamic_index_in_dim(blocks, (me + step + 4) % 4, 0, keepdims=False)

        total = block(0).astype(F32)
        for step in STEPS[1:]:
            total = total + hop(block(step), "y", step).astype(F32)
        total = total.astype(BF)
        every = [total] + [hop(total, "y", -step) for step in STEPS[1:]]
        factor = 1.0 / math.sqrt(ROWS * 128)

        def summed(t):
            step = (t - me + 4) % 4
            value = jnp.where(
                step == 0, every[0], jnp.where(step == 1, every[1], jnp.where(step == 3, every[2], every[3]))
            )
            return value.astype(F32) * factor

        qkv_grad = jnp.concatenate([summed(t) for t in range(3)], axis=1)
        out_grad = summed(3)
    return owner_rows, patch_grads, qkv_grad, out_grad


def solution(mesh):
    rows = P(("grp", "enc"), None)
    in_specs = (rows, P(), P("enc", None), P("enc", None), rows, rows, rows, rows)
    out_specs = (rows, rows, P("enc", None), P("enc", None))
    return jax.shard_map(body, mesh=mesh, in_specs=in_specs, out_specs=out_specs, check_vma=False)
```
